512 devices in a mesh: gx: 16 (over z_hi, x, core), gy: 32 (over y, z_lo).
Axes of the slice: x: 4, y: 4, z: 16 (z_hi: 2, z_lo: 8; z = z_hi * 8 + z_lo), core: 2. Of those that a mesh axis runs over, the one named last changes fastest.
Arguments:
- flow: float32 [5, 1024, 4096], P(None, 'gx', 'gy'), as said below
- vib: float32 [46, 1024, 4096], P(None, 'gx', 'gy'), may hold values from 0.2 to 2
- species: float32 [30, 1024, 4096], P(None, 'gx', 'gy'), may hold values from 0.2 to 2
- field_rate: float32 [1024, 4096], P('gx', 'gy'), may hold values from 0.25 to 2
- substeps: int32 [1024, 32], P('gx', 'gy'), may hold values from 2 to 16, as said below
- vib_rates: float32 [46, 46], replicated, as said below
- kin_rates: float32 [30, 30], replicated, as said below
- level_energy: float32 [46], replicated, may hold values from 0 to 0.05
- formation_heat: float32 [30], replicated, may hold values from 0 to 0.05
Outputs:
- new_flow: float32 [5, 1024, 4096], P(None, 'gx', 'gy')
- vib_final: float32 [46, 1024, 4096], P(None, 'gx', 'gy')
- species_final: float32 [30, 1024, 4096], P(None, 'gx', 'gy')
The draws below stay inside these ranges and needn't reach their ends.
Inputs may be any that keep to these rules, and one draw needn't show every extreme that they name: Blocks in the tile columns within 4 columns (periodic) of one column drawn from the seed take exactly 16 substeps; all others take 2 to 5. `flow`: density and pressure are at least 0.5 in every cell. `vib_rates`: diagonal entries between -2.5 and -1.5, off-diagonal ones between 0 and 1 / 46. `kin_rates`: diagonal entries between -2.5 and -1.5, off-diagonal ones between 0 and 1 / 30.
All inputs are finite; a program needn't handle non-finite values.
Results may differ from the reference program's by a relative error of at most 0.0001.
Values sent between devices are 32-bit elements; how exact they have to be, the bound alone decides.
No kernel may reach another device: no remote copies, remote signals or barrier semaphores. Data moves between devices by JAX's collectives and lax.ppermute only.
A program may use at most 64 MiB of HBM per device.

```python
import math
import jax
import jax.numpy as jnp
from jax import lax

LEVELS = 46
SPECIES = 30
RY = 128
MOST_STEPS = 16
NX = 1024
NY = 4096
COLS = 32


GAMMA = 1.4


def draw_flow(key, part):
    keys = jax.random.split(jax.random.fold_in(key, 3), 5)
    shape = (NX, NY)
    rho = jnp.exp(jax.random.uniform(keys[0], shape, jnp.float32, -0.69, 0.69))
    vel_a = jnp.clip(0.4 * jax.random.normal(keys[1], shape, jnp.float32), -1.0, 1.0)
    vel_b = jnp.clip(0.4 * jax.random.normal(keys[2], shape, jnp.float32), -1.0, 1.0)
    vel_c = jnp.clip(0.4 * jax.random.normal(keys[3], shape, jnp.float32), -1.0, 1.0)
    rho = jnp.maximum(rho, 0.5)
    press = jax.random.uniform(keys[4], shape, jnp.float32, 0.5, 2.0)
    energy = press / (GAMMA - 1.0) + 0.5 * rho * (vel_a * vel_a + vel_b * vel_b + vel_c * vel_c)
    return jnp.stack([rho, rho * vel_a, rho * vel_b, rho * vel_c, energy]).astype(jnp.float32)


def draw_substeps(key, part):
    key_a, key_b = jax.random.split(jax.random.fold_in(key, 11))
    center = jax.random.randint(key_a, (), 0, COLS)
    column = jnp.arange(COLS)
    apart = jnp.abs(column - center)
    apart = jnp.minimum(apart, COLS - apart)
    hot = apart <= COLS // 8
    cold = jax.random.randint(key_b, (NX, COLS), 2, 6)
    return jnp.where(hot[None, :], MOST_STEPS, cold).astype(jnp.int32)


def rate_matrix(key, order, low_share, jitter_top):
    key_a, key_b, key_c = jax.random.split(key, 3)
    off = jax.random.uniform(key_a, (order, order), jnp.float32, low_share / order, 1.0 / order)
    sign = jax.random.randint(key_b, (order,), 0, 2).astype(jnp.float32) * 2.0 - 1.0
    jitter = jax.random.uniform(key_c, (order,), jnp.float32, 0.0, 1.0) * jitter_top
    diag = -2.0 + sign * (0.5 - jitter)
    eye = jnp.eye(order, dtype=jnp.float32)
    return (off * (1.0 - eye) + eye * diag[:, None]).astype(jnp.float32)


def draw_vib_rates(key, part):
    key = jax.random.fold_in(key, 5)
    return rate_matrix(key, LEVELS, 0.85, 0.05)


def draw_kin_rates(key, part):
    key = jax.random.fold_in(key, 7)
    return rate_matrix(key, SPECIES, 0.85, 0.05)


def level_of(own_key, extent, shards, smallest, high):
    loudness = 1.0
    for axis_at, blocks in shards:
        steps = jax.random.uniform(jax.random.fold_in(jax.random.fold_in(own_key, 6), axis_at), (blocks,), jnp.float32, smallest / len(shards), high / len(shards))
        loudness = loudness * jnp.repeat(jnp.exp(steps), extent[axis_at] // blocks).reshape((-1,) + (1,) * (len(extent) - 1 - axis_at))
    return loudness


def setup_inputs(seed: int = 0) -> dict:
    key_of = jax.random.split(jax.random.key(seed), 10)
    flow = draw_flow(jax.random.fold_in(key_of[9], 71), 0)
    vib = jnp.clip(jnp.exp(math.log(2.0) - 2.3025851 * jax.random.uniform(key_of[1], (LEVELS, NX, NY), jnp.float32) ** level_of(key_of[1], (LEVELS, NX, NY), ((1, 16), (2, 32)), -0.2, 0.2)), 0.2, 2.0)
    species = jnp.clip(jnp.exp(math.log(2.0) - 2.3025851 * jax.random.uniform(key_of[2], (SPECIES, NX, NY), jnp.float32) ** level_of(key_of[2], (SPECIES, NX, NY), ((1, 16), (2, 32)), -0.2, 0.2)), 0.2, 2.0)
    field_rate = jnp.clip(jnp.exp(math.log(2.0) - 2.0794415 * jax.random.uniform(key_of[3], (NX, NY), jnp.float32) ** level_of(key_of[3], (NX, NY), ((0, 16), (1, 32)), -0.2, 0.2)), 0.25, 2.0)
    substeps = draw_substeps(jax.random.fold_in(key_of[9], 71), 0)
    vib_rates = draw_vib_rates(jax.random.fold_in(key_of[9], 71), 0)
    kin_rates = draw_kin_rates(jax.random.fold_in(key_of[9], 71), 0)
    level_energy = jnp.clip(jax.random.uniform(key_of[7], (LEVELS,), jnp.float32, 0.0, 0.05), 0.0, 0.05)
    formation_heat = jnp.clip(jax.random.uniform(key_of[8], (SPECIES,), jnp.float32, 0.0, 0.05), 0.0, 0.05)
    return {"flow": flow, "vib": vib, "species": species, "field_rate": field_rate, "substeps": substeps, "vib_rates": vib_rates, "kin_rates": kin_rates, "level_energy": level_energy, "formation_heat": formation_heat}


GAMMA = 1.4
COURANT = 0.1
H_CHEM = 0.05
EPS_W = 1e-06
HIGH = lax.Precision.HIGHEST

def fluxes(q):
    rho = q[0]
    speed_u = q[1] / rho
    kinetic = 0.5 * (q[1] * q[1] + q[2] * q[2] + q[3] * q[3]) / rho
    press = (GAMMA - 1.0) * (q[4] - kinetic)
    flux = jnp.stack([q[1], q[1] * speed_u + press, q[2] * speed_u, q[3] * speed_u, (q[4] + press) * speed_u])
    speed = jnp.abs(speed_u) + jnp.sqrt(GAMMA * press / rho)
    return (flux, speed)

def weno_face(v0, v1, v2, v3, v4):
    p0 = (2.0 * v0 - 7.0 * v1 + 11.0 * v2) / 6.0
    p1 = (-v1 + 5.0 * v2 + 2.0 * v3) / 6.0
    p2 = (2.0 * v2 + 5.0 * v3 - v4) / 6.0
    b0 = 13.0 / 12.0 * (v0 - 2.0 * v1 + v2) ** 2 + 0.25 * (v0 - 4.0 * v1 + 3.0 * v2) ** 2
    b1 = 13.0 / 12.0 * (v1 - 2.0 * v2 + v3) ** 2 + 0.25 * (v1 - v3) ** 2
    b2 = 13.0 / 12.0 * (v2 - 2.0 * v3 + v4) ** 2 + 0.25 * (3.0 * v2 - 4.0 * v3 + v4) ** 2
    a0 = 0.1 / (EPS_W + b0) ** 2
    a1 = 0.6 / (EPS_W + b1) ** 2
    a2 = 0.3 / (EPS_W + b2) ** 2
    return (a0 * p0 + a1 * p1 + a2 * p2) / (a0 + a1 + a2)

def divergence(q):
    count = q.shape[1] - 6
    flux, speed = fluxes(q)
    speed3 = speed[None]

    def take(arr, offset):
        return arr[:, offset:offset + count + 1]
    alpha = take(speed3, 0)
    for offset in range(1, 6):
        alpha = jnp.maximum(alpha, take(speed3, offset))
    plus = [0.5 * (take(flux, o) + alpha * take(q, o)) for o in range(0, 5)]
    minus = [0.5 * (take(flux, o) - alpha * take(q, o)) for o in range(1, 6)]
    face = weno_face(*plus) + weno_face(minus[4], minus[3], minus[2], minus[1], minus[0])
    return face[:, 1:] - face[:, :-1]

def permute(q):
    return jnp.stack([q[0], q[2], q[1], q[3], q[4]])

def advance(padded):
    along_x = divergence(padded[:, :, 3:-3])
    turned = permute(jnp.swapaxes(padded[:, 3:-3, :], 1, 2))
    along_y = jnp.swapaxes(permute(divergence(turned)), 1, 2)
    return padded[:, 3:-3, 3:-3] - COURANT * (along_x + along_y)

def reference(flow, vib, species, field_rate, substeps, vib_rates, kin_rates, level_energy, formation_heat):
    cell_counts = jnp.repeat(substeps, RY, axis=1)

    def substep(k, state):
        levels, dens = state
        live = k < cell_counts
        prod_v = jnp.einsum('lm,mxy->lxy', vib_rates, levels, precision=HIGH)
        prod_s = jnp.einsum('lm,mxy->lxy', kin_rates, dens, precision=HIGH)
        levels = jnp.where(live, levels + H_CHEM * (field_rate * prod_v), levels)
        dens = jnp.where(live, dens + H_CHEM * (field_rate * prod_s), dens)
        return (levels, dens)
    vib_final, species_final = lax.fori_loop(0, MOST_STEPS, substep, (vib, species))
    heat = jnp.einsum('l,lxy->xy', level_energy, vib - vib_final, precision=HIGH)
    heat = heat + jnp.einsum('l,lxy->xy', formation_heat, species - species_final, precision=HIGH)
    heated = jnp.concatenate([flow[:4], (flow[4] + heat)[None]], 0)
    padded = jnp.pad(heated, ((0, 0), (3, 3), (3, 3)), mode='wrap')
    return (advance(padded), vib_final, species_final)
```

```python
import jax
import jax.numpy as jnp
from jax import lax
from jax.experimental import pallas as pl
from jax.experimental.pallas import tpu as pltpu
from jax.sharding import PartitionSpec as P

F32, BF16 = jnp.float32, jnp.bfloat16
HIGH = lax.Precision.HIGHEST
VO = (0, 8, 16, 24, 32, 38)
SO = (0, 8, 16, 22)
R = 8


def widen_rates(vr_ref, kr_ref, va, sa):
    va[...] = jnp.zeros_like(va)
    sa[...] = jnp.zeros_like(sa)
    va[0:40, 0:46] = vr_ref[0:40, :]
    va[40:48, 0:46] = vr_ref[38:46, :]
    sa[0:24, 0:30] = kr_ref[0:24, :]
    sa[24:32, 0:30] = kr_ref[22:30, :]
    v = va[...]
    s = sa[...]
    lane = lax.broadcasted_iota(jnp.int32, (48, 128), 1)
    v = jnp.where(lane < 38, v, jnp.where((lane >= 40) & (lane < 48), pltpu.roll(v, 2, 1), 0.0))
    lane = lax.broadcasted_iota(jnp.int32, (32, 128), 1)
    s = jnp.where(
        (lane >= 48) & (lane < 70),
        pltpu.roll(s, 48, 1),
        jnp.where((lane >= 72) & (lane < 80), pltpu.roll(s, 50, 1), 0.0),
    )
    b = jnp.concatenate([v, s, jnp.zeros((48, 128), F32)], 0)
    row = lax.broadcasted_iota(jnp.int32, (128, 128), 0)
    col = lax.broadcasted_iota(jnp.int32, (128, 128), 1)
    rid = jnp.where(row < 40, row, jnp.where(row < 48, row - 2, jnp.where(row < 72, row + 52, row + 50)))
    cid = jnp.where(
        col < 38,
        col,
        jnp.where(
            (col >= 40) & (col < 48),
            col - 2,
            jnp.where((col >= 48) & (col < 70), col + 52, jnp.where((col >= 72) & (col < 80), col + 50, -1)),
        ),
    )
    return b + jnp.where((rid == cid) & (row < 80), 2.0, 0.0)


def pack_split(m):
    hi = m.astype(BF16).astype(F32)
    lo = m - hi
    lane = lax.broadcasted_iota(jnp.int32, m.shape, 1)
    first = jnp.where(lane < 80, hi, pltpu.roll(hi, 80, 1))
    second = jnp.where(lane < 32, pltpu.roll(hi, 80, 1), pltpu.roll(lo, 32, 1))
    return jnp.concatenate([first, second], 1).astype(BF16)


def powers(vr_ref, kr_ref, va, sa, w_scr, w8_scr):
    def mm(a, b):
        return jnp.dot(a, b, precision=HIGH, preferred_element_type=F32)

    b1 = widen_rates(vr_ref, kr_ref, va, sa)
    b2 = mm(b1, b1)
    b3 = mm(b2, b1)
    b4 = mm(b2, b2)
    b5 = mm(b4, b1)
    b6 = mm(b4, b2)
    b7 = mm(b4, b3)
    b8 = mm(b4, b4)
    for j, m in enumerate((b1, b2, b3, b4, b5, b6, b7, b8)):
        w_scr[80 * j : 80 * j + 80, :] = pack_split(m[0:80])
    w8_scr[...] = b8[0:80].astype(BF16)


def coefs(rate, n, s_scr):
    hr = 0.05 * rate
    a = 1.0 - 2.0 * hr
    t = hr / a
    s = n * t
    s_scr[0] = s
    for j in range(1, 16):
        s = s * (((n - j) * (1.0 / (j + 1))) * t)
        s_scr[j] = s
    m = n.astype(jnp.int32)
    p = jnp.ones_like(a)
    q = a
    for k in range(5):
        p = jnp.where(((m >> k) & 1) == 1, p * q, p)
        if k < 4:
            q = q * q
    s_scr[16] = p


def chem_kernel(vr_ref, kr_ref, ev_ref, es_ref, vib_ref, sp_ref, rate_ref, cnt_ref, flow_ref,
                vo_ref, so_ref, e_ref, xa_ref, xb_ref, ya_ref, yb_ref, own_ref, va, sa, w_scr, w8_scr, s_scr, p_scr, y_scr, y1_scr):
    @pl.when(pl.program_id(0) == 0)
    def _():
        powers(vr_ref, kr_ref, va, sa, w_scr, w8_scr)

    g = pl.program_id(0)
    row = lax.broadcasted_iota(jnp.int32, (R, 128), 0)
    n = jnp.zeros((R, 128), jnp.int32)
    for r in range(R):
        n = jnp.where(row == r, cnt_ref[g * R + r], n)
    n = n.astype(F32)
    coefs(rate_ref[...], n, s_scr)
    v2 = vib_ref.reshape(46 * R, 128)
    s2 = sp_ref.reshape(30 * R, 128)
    vo2 = vo_ref.reshape(46 * R, 128)
    so2 = so_ref.reshape(30 * R, 128)

    def cf(i, j):
        return jnp.concatenate([s_scr[j - 1, pl.ds(2 * i, 1), :], s_scr[j - 1, pl.ds(2 * i + 1, 1), :]], 1)

    def load(i):
        def col(r):
            return jnp.concatenate(
                [v2[pl.ds(o * R + r, 8, stride=R), :] for o in VO]
                + [s2[pl.ds(o * R + r, 8, stride=R), :] for o in SO], 0)

        return jnp.concatenate([col(2 * i), col(2 * i + 1)], 1)

    def expand(i):
        x = load(i)
        hi = x.astype(BF16)
        lo = (x - hi.astype(F32)).astype(BF16)
        xk = jnp.concatenate([hi, lo, hi, jnp.zeros((16, 256), BF16)], 0)
        p_scr[i % 2] = jnp.dot(w_scr[...], xk, preferred_element_type=F32)

    def combine(i):
        x = load(i)
        y0 = x
        y1 = cf(i, 8) * x
        for j in range(1, 9):
            w = p_scr[i % 2, 80 * (j - 1) : 80 * j, :]
            if j < 8:
                y0 = y0 + cf(i, j) * w
            y1 = y1 + cf(i, 8 + j) * w
        y_scr[i % 2] = y0
        y1_scr[i % 2] = jnp.concatenate([y1.astype(BF16), jnp.zeros((48, 256), BF16)], 0)

    def finish(i):
        z = jnp.dot(w8_scr[...], y1_scr[i % 2], preferred_element_type=F32)
        out = cf(i, 17) * (y_scr[i % 2] + z)
        for h in range(2):
            r = 2 * i + h
            for k, o in enumerate(VO):
                vo2[pl.ds(o * R + r, 8, stride=R), :] = out[8 * k : 8 * k + 8, 128 * h : 128 * h + 128]
            for k, o in enumerate(SO):
                so2[pl.ds(o * R + r, 8, stride=R), :] = out[48 + 8 * k : 56 + 8 * k, 128 * h : 128 * h + 128]

    NP = R // 2
    for i in range(NP + 2):
        if i < NP:
            expand(i)
        if 0 <= i - 2 < NP:
            finish(i - 2)
        if 0 <= i - 1 < NP:
            combine(i - 1)
    acc = flow_ref[4]
    for l in range(46):
        acc = acc + ev_ref[l] * (vib_ref[l] - vo_ref[l])
    for l in range(30):
        acc = acc + es_ref[l] * (sp_ref[l] - so_ref[l])
    e_ref[...] = acc


    q = [flow_ref[0], flow_ref[1], flow_ref[2], flow_ref[3], acc]
    even_x = lax.axis_index("gx") % 2 == 0
    even_y = lax.axis_index("gy") % 2 == 0

    def rows_to(ref, lo):
        for c in range(5):
            ref[3 * c : 3 * c + 3, :] = q[c][lo : lo + 3, :]
        ref[15:16, :] = jnp.ones((1, 128), F32)

    first, last = g == 0, g == pl.num_programs(0) - 1
    pl.when(first & even_x)(lambda: rows_to(xb_ref, 0))
    pl.when(first & ~even_x)(lambda: rows_to(xa_ref, 0))
    pl.when(last & even_x)(lambda: rows_to(xa_ref, R - 3))
    pl.when(last & ~even_x)(lambda: rows_to(xb_ref, R - 3))

    @pl.when(first)
    def _():
        for ref in (ya_ref, yb_ref, own_ref):
            ref[...] = jnp.ones((8, 128), F32)

    lane = lax.broadcasted_iota(jnp.int32, (8, 128), 1)
    left = own_ref[...]
    right = jnp.where(even_y, ya_ref[...], yb_ref[...])
    for c in range(5):
        at = 16 * g + 3 * c
        here = (lane >= at) & (lane < at + 3)
        left = jnp.where(here, pltpu.roll(q[c], at, 1), left)
        right = jnp.where(here, pltpu.roll(q[c], (at + 3) % 128, 1), right)
    own_ref[...] = left
    ya_ref[...] = jnp.where(even_y, right, left)
    yb_ref[...] = jnp.where(even_y, left, right)


def chem(flow, vib, sp, rate, cnt, vr, kr, ev, es, rows=64):
    full = lambda shape: pl.BlockSpec(shape, lambda i: (0,) * len(shape))
    smem = pl.BlockSpec(memory_space=pltpu.SMEM)
    return pl.pallas_call(
        chem_kernel,
        grid=(rows // R,),
        in_specs=[full((46, 46)), full((30, 30)), smem, smem,
                  pl.BlockSpec((46, R, 128), lambda i: (0, i, 0)),
                  pl.BlockSpec((30, R, 128), lambda i: (0, i, 0)),
                  pl.BlockSpec((R, 128), lambda i: (i, 0)),
                  smem,
                  pl.BlockSpec((5, R, 128), lambda i: (0, i, 0))],
        out_specs=[pl.BlockSpec((46, R, 128), lambda i: (0, i, 0)),
                   pl.BlockSpec((30, R, 128), lambda i: (0, i, 0)),
                   pl.BlockSpec((R, 128), lambda i: (i, 0)),
                   full((16, 128)), full((16, 128)), full((8, 128)), full((8, 128)), full((8, 128))],
        out_shape=[jax.ShapeDtypeStruct((46, rows, 128), F32), jax.ShapeDtypeStruct((30, rows, 128), F32),
                   jax.ShapeDtypeStruct((rows, 128), F32)]
        + [jax.ShapeDtypeStruct((k, 128), F32) for k in (16, 16, 8, 8, 8)],
        scratch_shapes=[pltpu.VMEM((48, 128), F32), pltpu.VMEM((32, 128), F32),
                        pltpu.VMEM((640, 256), BF16), pltpu.VMEM((80, 128), BF16),
                        pltpu.VMEM((17, R, 128), F32), pltpu.VMEM((2, 640, 256), F32),
                        pltpu.VMEM((2, 80, 256), F32), pltpu.VMEM((2, 128, 256), BF16)],
        compiler_params=pltpu.CompilerParams(vmem_limit_bytes=62 * 2**20),
        cost_estimate=pl.CostEstimate(flops=10**9, bytes_accessed=6 * 10**6, transcendentals=0),
        name="chemistry",
    )(vr, kr, ev, es, vib, sp, rate, cnt, flow)


def cell_flux(q, d):
    inv = 1.0 / q[0]
    u = q[d] * inv
    p = 0.4 * (q[4] - 0.5 * (q[1] * q[1] + q[2] * q[2] + q[3] * q[3]) * inv)
    f = [q[0] * u, q[1] * u, q[2] * u, q[3] * u, (q[4] + p) * u]
    f[d] = f[d] + p
    return f, jnp.abs(u) + jnp.sqrt(1.4 * p * inv)


def recip(v):
    return pl.reciprocal(v, approx=True)


def side(v2, d0, d1, d2, d3):
    c0, c1, c2 = d1 - d0, d2 - d1, d3 - d2
    t1 = 3.0 * d1
    e0 = t1 - d0
    e1 = d1 + d2
    e2 = d3 - 3.0 * d2
    k = 13.0 / 3.0
    s0 = 1.6e-5 + (k * (c0 * c0) + e0 * e0)
    s1 = 1.6e-5 + (k * (c1 * c1) + e1 * e1)
    s2 = 1.6e-5 + (k * (c2 * c2) + e2 * e2)
    r0, r1, r2 = recip(s0), recip(s1), recip(s2)
    a0 = r0 * r0
    a1 = 6.0 * (r1 * r1)
    a2 = 3.0 * (r2 * r2)
    num = a0 * ((c0 + c0) + t1) + a1 * (e1 + d2) + a2 * (d2 - e2)
    den = a0 + a1 + a2
    return v2 + num / (6.0 * den)


def face(f, q, alpha):
    fd = [f[k + 1] - f[k] for k in range(5)]
    qd = [alpha * (q[k + 1] - q[k]) for k in range(5)]
    plus = side(f[2] + alpha * q[2], *[fd[k] + qd[k] for k in range(4)])
    m = [qd[k] - fd[k] for k in range(5)]
    minus = side(f[3] - alpha * q[3], m[4], m[3], m[2], m[1])
    return plus + minus


def weno_kernel(flow_ref, e_ref, xa_ref, xb_ref, ya_ref, yb_ref, own_ref, out_ref, xq, xf, xs, xg):
    even_x = lax.axis_index("gx") % 2 == 0
    even_y = lax.axis_index("gy") % 2 == 0
    xa, xb, ya, yb = xa_ref[...], xb_ref[...], ya_ref[...], yb_ref[...]
    up, dn = jnp.where(even_x, xb, xa), jnp.where(even_x, xa, xb)
    lq, rq = jnp.where(even_y, yb, ya), jnp.where(even_y, ya, yb)
    for c in range(5):
        xq[c, 5:8, :] = up[3 * c : 3 * c + 3, :]
        xq[c, 8:72, :] = e_ref[...] if c == 4 else flow_ref[c]
        xq[c, 72:75, :] = dn[3 * c : 3 * c + 3, :]
    one = jnp.ones((5, 128), F32)
    for c in range(5):
        fill = one if c in (0, 4) else 0.0 * one
        xq[c, 0:5, :] = fill
        xq[c, 75:80, :] = fill
    for g in range(10):
        sl = slice(8 * g, 8 * g + 8)
        f, s = cell_flux([xq[c, sl, :] for c in range(5)], 1)
        for c in range(5):
            xf[c, sl, :] = f[c]
        xs[sl, :] = s
    for g in range(9):
        b = 8 * g + 5
        n = 8 if g < 8 else 1
        alpha = xs[b : b + n, :]
        for o in range(1, 6):
            alpha = jnp.maximum(alpha, xs[b + o : b + o + n, :])
        for c in range(5):
            xg[c, 8 * g : 8 * g + n, :] = face(
                [xf[c, b + o : b + o + n, :] for o in range(6)],
                [xq[c, b + o : b + o + n, :] for o in range(6)],
                alpha,
            )

    lane = lax.broadcasted_iota(jnp.int32, (8, 128), 1)
    slot = lane % 16

    def shift(v, k):
        return v if k % 128 == 0 else pltpu.roll(v, (-k) % 128, 1)

    def strip(v):
        q = [shift(v, 3 * c) for c in range(5)]
        f, s = cell_flux(q, 2)
        ff = f[0]
        ss = s
        for c in range(1, 5):
            here = slot >= 3 * c
            ff = jnp.where(here, shift(f[c], -3 * c), ff)
            ss = jnp.where(here, shift(s, -3 * c), ss)
        return v, ff, ss

    lq, lfx, ls = strip(lq)
    oq, ofx, os_ = strip(own_ref[...])
    alpha = ls
    for v in (shift(ls, 1), shift(ls, 2), os_, shift(os_, 1), shift(os_, 2)):
        alpha = jnp.maximum(alpha, v)
    first = face(
        [lfx, shift(lfx, 1), shift(lfx, 2), ofx, shift(ofx, 1), shift(ofx, 2)],
        [lq, shift(lq, 1), shift(lq, 2), oq, shift(oq, 1), shift(oq, 2)],
        alpha,
    )
    for g in range(8):
        sl = slice(8 * g + 8, 8 * g + 16)
        q = [xq[c, sl, :] for c in range(5)]
        h = [
            jnp.where(lane < 64, shift(rq, 16 * g + 3 * c), shift(lq, 16 * g + 3 * c - 125)) for c in range(5)
        ]
        f, s = cell_flux(q, 2)
        hf, hs = cell_flux(h, 2)

        def six(a, b):
            out = []
            for o in range(-2, 4):
                if o == 0:
                    out.append(a)
                elif o > 0:
                    out.append(shift(jnp.where(lane < o, b, a), o))
                else:
                    out.append(shift(jnp.where(lane >= 128 + o, b, a), o))
            return out

        alphas = six(s, hs)
        alpha = alphas[0]
        for v in alphas[1:]:
            alpha = jnp.maximum(alpha, v)
        for c in range(5):
            after = face(six(f[c], hf[c]), six(q[c], h[c]), alpha)
            before = jnp.where(lane == 0, shift(first, 16 * g + 3 * c), shift(after, -1))
            gx = xg[c, 8 * g + 1 : 8 * g + 9, :] - xg[c, 8 * g : 8 * g + 8, :]
            out_ref[c, 8 * g : 8 * g + 8, :] = q[c] - 0.05 * (gx + (after - before))


def weno(flow, e, xa, xb, ya, yb, own):
    vm = pl.BlockSpec(memory_space=pltpu.VMEM)
    return pl.pallas_call(
        weno_kernel,
        in_specs=[vm] * 7,
        out_specs=vm,
        out_shape=jax.ShapeDtypeStruct((5, 64, 128), F32),
        scratch_shapes=[pltpu.VMEM((5, 80, 128), F32), pltpu.VMEM((5, 80, 128), F32), pltpu.VMEM((80, 128), F32),
                        pltpu.VMEM((5, 72, 128), F32)],
        compiler_params=pltpu.CompilerParams(vmem_limit_bytes=62 * 2**20),
        cost_estimate=pl.CostEstimate(flops=10**7, bytes_accessed=10**6, transcendentals=0),
        name="euler_weno",
    )(flow, e, xa, xb, ya, yb, own)


def swaps(size, start):
    pairs = [(i % size, (i + 1) % size) for i in range(start, size, 2)]
    return pairs + [(b, a) for a, b in pairs]


def swapped(value, axis, start):
    return lax.ppermute(value, axis, swaps(lax.axis_size(axis), start))


def local(flow, vib, species, field_rate, substeps, vib_rates, kin_rates, level_energy, formation_heat):
    vib_final, species_final, e, xa, xb, ya, yb, own = chem(
        flow, vib, species, field_rate, substeps.reshape(-1), vib_rates, kin_rates, level_energy, formation_heat
    )
    ya = swapped(ya, "gy", 0)
    yb = swapped(yb, "gy", 1)
    xa = swapped(xa, "gx", 0)
    xb = swapped(xb, "gx", 1)
    return (weno(flow, e, xa, xb, ya, yb, own), vib_final, species_final)


def solution(mesh):
    tiled = P(None, "gx", "gy")
    return jax.shard_map(
        local,
        mesh=mesh,
        in_specs=(tiled, tiled, tiled, P("gx", "gy"), P("gx", "gy"), P(), P(), P(), P()),
        out_specs=(tiled, tiled, tiled),
        check_vma=False,
    )
```

```python
import functools

import jax
import jax.numpy as jnp
from jax import lax
from jax.experimental import pallas as pl
from jax.experimental.pallas import tpu as pltpu
from jax.sharding import PartitionSpec as P

F32, BF16 = jnp.float32, jnp.bfloat16
HIGH = lax.Precision.HIGHEST
VO = (0, 8, 16, 24, 32, 38)
SO = (0, 8, 16, 22)


def widen_rates(vr_ref, kr_ref, va, sa):
    va[...] = jnp.zeros_like(va)
    sa[...] = jnp.zeros_like(sa)
    va[0:40, 0:46] = vr_ref[0:40, :]
    va[40:48, 0:46] = vr_ref[38:46, :]
    sa[0:24, 0:30] = kr_ref[0:24, :]
    sa[24:32, 0:30] = kr_ref[22:30, :]
    v = va[...]
    s = sa[...]
    lane = lax.broadcasted_iota(jnp.int32, (48, 128), 1)
    v = jnp.where(lane < 38, v, jnp.where((lane >= 40) & (lane < 48), pltpu.roll(v, 2, 1), 0.0))
    lane = lax.broadcasted_iota(jnp.int32, (32, 128), 1)
    s = jnp.where(
        (lane >= 48) & (lane < 70),
        pltpu.roll(s, 48, 1),
        jnp.where((lane >= 72) & (lane < 80), pltpu.roll(s, 50, 1), 0.0),
    )
    b = jnp.concatenate([v, s, jnp.zeros((48, 128), F32)], 0)
    row = lax.broadcasted_iota(jnp.int32, (128, 128), 0)
    col = lax.broadcasted_iota(jnp.int32, (128, 128), 1)
    rid = jnp.where(row < 40, row, jnp.where(row < 48, row - 2, jnp.where(row < 72, row + 52, row + 50)))
    cid = jnp.where(
        col < 38,
        col,
        jnp.where(
            (col >= 40) & (col < 48),
            col - 2,
            jnp.where((col >= 48) & (col < 70), col + 52, jnp.where((col >= 72) & (col < 80), col + 50, -1)),
        ),
    )
    return b + jnp.where((rid == cid) & (row < 80), 2.0, 0.0)


def pack_split(m):
    hi = m.astype(BF16).astype(F32)
    lo = m - hi
    lane = lax.broadcasted_iota(jnp.int32, m.shape, 1)
    first = jnp.where(lane < 80, hi, pltpu.roll(hi, 80, 1))
    second = jnp.where(lane < 32, pltpu.roll(hi, 80, 1), pltpu.roll(lo, 32, 1))
    return jnp.concatenate([first, second], 1).astype(BF16)


def mm(a, b):
    return jnp.dot(a, b, precision=HIGH, preferred_element_type=F32)


def load_pair(v2, s2, g, k):
    def one(r):
        return jnp.concatenate(
            [v2[pl.ds(g * 368 + (o * 8 + r), 8, stride=8), :] for o in VO]
            + [s2[pl.ds(g * 240 + (o * 8 + r), 8, stride=8), :] for o in SO], 0)

    return jnp.concatenate([one(2 * k), one(2 * k + 1)], 1)


def split_stack(x):
    hi = x.astype(BF16)
    lo = (x - hi.astype(F32)).astype(BF16)
    return jnp.concatenate([hi, lo, hi, jnp.zeros((16, 256), BF16)], 0)


def group_counts(cnt_ref, g):
    row = lax.broadcasted_iota(jnp.int32, (8, 128), 0)
    n = jnp.zeros((8, 128), jnp.int32)
    for r in range(8):
        n = jnp.where(row == r, cnt_ref[g * 8 + r], n)
    return n.astype(F32)


def heat_kernel(vr_hbm, kr_hbm, ev_hbm, es_hbm, cnt_hbm, rate_hbm, flow_hbm, vib_hbm, sp_hbm,
                e_ref, xa_ref, xb_ref, ya_ref, yb_ref, own_ref,
                vr_ref, kr_ref, ev_ref, es_ref, cnt_ref, rate_ref, flow_ref,
                vib, sp, va, sa, ee, g_scr, s_scr, p_scr, w_scr, sems, wsem):
    small = [pltpu.make_async_copy(a, b, wsem.at[k])
             for k, (a, b) in enumerate(((vr_hbm, vr_ref), (kr_hbm, kr_ref), (ev_hbm, ev_ref), (es_hbm, es_ref),
                                         (cnt_hbm, cnt_ref), (rate_hbm, rate_ref), (flow_hbm, flow_ref)))]
    for c in small[:6]:
        c.start()

    def pieces(g):
        sl = pl.ds(pl.multiple_of(8 * g, 8), 8)
        return (pltpu.make_async_copy(vib_hbm.at[:, sl, :], vib.at[g], sems.at[0, g]),
                pltpu.make_async_copy(sp_hbm.at[:, sl, :], sp.at[g], sems.at[1, g]))

    for g in range(8):
        for c in pieces(g):
            c.start()
    small[6].start()
    for c in small[:6]:
        c.wait()
    for g in range(8):
        coefs(rate_ref[8 * g : 8 * g + 8, :], group_counts(cnt_ref, g), s_scr, 8 * g)

    b1 = widen_rates(vr_ref, kr_ref, va, sa)
    ee[...] = jnp.zeros_like(ee)
    ee[0:1, 0:46] = ev_ref[...]
    ee[8:9, 0:30] = es_ref[...]
    lane = lax.broadcasted_iota(jnp.int32, (8, 128), 1)
    v, s = ee[0:8, :], ee[8:16, :]
    v = jnp.where(lane < 38, v, jnp.where((lane >= 40) & (lane < 48), pltpu.roll(v, 2, 1), 0.0))
    v = jnp.where((lane >= 48) & (lane < 70), pltpu.roll(s, 48, 1),
                  jnp.where((lane >= 72) & (lane < 80), pltpu.roll(s, 50, 1), v))
    G = jnp.concatenate([v, jnp.zeros((24, 128), F32)], 0)
    b2 = mm(b1, b1)
    G = G + pltpu.roll(mm(G, b1), 1, 0)
    b4 = mm(b2, b2)
    G = G + pltpu.roll(mm(G, b2), 2, 0)
    b8 = mm(b4, b4)
    G = G + pltpu.roll(mm(G, b4), 4, 0)
    G = G + pltpu.roll(mm(G, b8), 8, 0)
    row = lax.broadcasted_iota(jnp.int32, (32, 128), 0)
    G = G + jnp.where(row == 16, pltpu.roll(mm(G, b8), 8, 0), 0.0)
    g_scr[...] = pack_split(G)

    v2 = vib.reshape(8 * 368, 128)
    s2 = sp.reshape(8 * 240, 128)
    even_x = lax.axis_index("gx") % 2 == 0
    even_y = lax.axis_index("gy") % 2 == 0
    small[6].wait()

    def sums(g, left, right):
        sl = pl.ds(pl.multiple_of(8 * g, 8), 8)
        first = p_scr[pl.ds(192 * g, 8, stride=24), :]
        acc = first
        for j in range(1, 17):
            acc = acc + s_scr[j - 1, sl, :] * p_scr[pl.ds(192 * g + j, 8, stride=24), :]
        e = flow_ref[4, sl, :] + (first - s_scr[16, sl, :] * acc)
        e_ref[sl, :] = e
        for c in range(5):
            at = 16 * g + 3 * c
            v = e if c == 4 else flow_ref[c, sl, :]
            here = (lane >= at) & (lane < at + 3)
            left = jnp.where(here, pltpu.roll(v, at, 1), left)
            right = jnp.where(here, pltpu.roll(v, lax.rem(at + 3, 128), 1), right)
        return left, right

    p_scr[0:192, :] = jnp.zeros((192, 128), F32)

    def turn(g, carry):
        for c in pieces(g):
            c.wait()
        for i in range(4):
            r = 8 * g + 2 * i
            w = jnp.dot(g_scr[...], split_stack(load_pair(v2, s2, g, i)), preferred_element_type=F32)
            w_scr[48 * i : 48 * i + 24, :] = w[0:24, 0:128]
            w_scr[48 * i + 24 : 48 * i + 48, :] = w[0:24, 128:256]
        out = sums(jnp.maximum(g - 1, 0), *carry)
        p_scr[pl.ds(pl.multiple_of(192 * g, 8), 192), :] = w_scr[...]
        return out

    left = jnp.ones((8, 128), F32)
    left, right = lax.fori_loop(0, 8, turn, (left, left))
    left, right = sums(7, left, right)
    edge = {}
    for g in (0, 7):
        sl = slice(8 * g, 8 * g + 8)
        edge[g] = [flow_ref[c, sl, :] for c in range(4)] + [e_ref[sl, :]]
    own_ref[...] = left
    ya_ref[0:8, :] = jnp.where(even_y, right, left)
    yb_ref[0:8, :] = jnp.where(even_y, left, right)
    ya_ref[8:16, :] = jnp.ones((8, 128), F32)
    yb_ref[8:16, :] = jnp.ones((8, 128), F32)
    for c in range(5):
        top, bottom = edge[0][c][0:3, :], edge[7][c][5:8, :]
        xa_ref[3 * c : 3 * c + 3, :] = jnp.where(even_x, bottom, top)
        xb_ref[3 * c : 3 * c + 3, :] = jnp.where(even_x, top, bottom)
    xa_ref[15:16, :] = jnp.ones((1, 128), F32)
    xb_ref[15:16, :] = jnp.ones((1, 128), F32)


def heat(flow, vib, sp, rate, cnt, vr, kr, ev, es):
    vm = pl.BlockSpec(memory_space=pltpu.VMEM)
    hbm = pl.BlockSpec(memory_space=pl.ANY)
    return pl.pallas_call(
        heat_kernel,
        in_specs=[hbm] * 9,
        out_specs=[vm] * 6,
        out_shape=[jax.ShapeDtypeStruct((k, 128), F32) for k in (64, 16, 16, 16, 16, 8)],
        scratch_shapes=[pltpu.VMEM((46, 46), F32), pltpu.VMEM((30, 30), F32), pltpu.VMEM((1, 46), F32),
                        pltpu.VMEM((1, 30), F32), pltpu.SMEM((64,), jnp.int32), pltpu.VMEM((64, 128), F32),
                        pltpu.VMEM((5, 64, 128), F32),
                        pltpu.VMEM((8, 46, 8, 128), F32), pltpu.VMEM((8, 30, 8, 128), F32),
                        pltpu.VMEM((48, 128), F32), pltpu.VMEM((32, 128), F32), pltpu.VMEM((16, 128), F32),
                        pltpu.VMEM((32, 256), BF16), pltpu.VMEM((17, 64, 128), F32), pltpu.VMEM((1536, 128), F32),
                        pltpu.VMEM((192, 128), F32),
                        pltpu.SemaphoreType.DMA((2, 8)), pltpu.SemaphoreType.DMA((7,))],
        compiler_params=pltpu.CompilerParams(vmem_limit_bytes=62 * 2**20),
        cost_estimate=pl.CostEstimate(flops=10**8, bytes_accessed=3 * 10**6, transcendentals=0),
        name="heat",
    )(vr, kr, ev.reshape(1, -1), es.reshape(1, -1), cnt, rate, flow, vib, sp)


def powers(vr_ref, kr_ref, va, sa, w_scr, w8_scr):
    b1 = widen_rates(vr_ref, kr_ref, va, sa)
    b2 = mm(b1, b1)
    b3 = mm(b2, b1)
    b4 = mm(b2, b2)
    b5 = mm(b4, b1)
    b6 = mm(b4, b2)
    b7 = mm(b4, b3)
    b8 = mm(b4, b4)
    for j, m in enumerate((b1, b2, b3, b4, b5, b6, b7, b8)):
        w_scr[80 * j : 80 * j + 80, :] = pack_split(m[0:80])
    w8_scr[...] = b8[0:80].astype(BF16)


def coefs(rate, n, s_scr, at):
    hr = 0.05 * rate
    a = 1.0 - 2.0 * hr
    t = hr / a
    s = n * t
    s_scr[0, at : at + 8, :] = s
    for j in range(1, 16):
        s = s * (((n - j) * (1.0 / (j + 1))) * t)
        s_scr[j, at : at + 8, :] = s
    m = n.astype(jnp.int32)
    p = jnp.ones_like(a)
    q = a
    for k in range(5):
        p = jnp.where(((m >> k) & 1) == 1, p * q, p)
        if k < 4:
            q = q * q
    s_scr[16, at : at + 8, :] = p


def chem_kernel(early, vr_hbm, kr_hbm, cnt_hbm, rate_hbm, vib_hbm, sp_hbm, *rest):
    vo_hbm, so_hbm = rest[4:6] if early else rest[2:4]
    vr, kr, cnt, rate, vib, sp, vo, so, va, sa, w_scr, w8_scr, s_scr, p_scr, y_scr, y1_scr, sems, osems, wsem = rest[-19:]
    half = lax.axis_size("gx") // 2

    @pl.when(((lax.axis_index("gx") < half) & (lax.axis_index("gy") % 8 < 4)) == early)
    def _():
        small = [pltpu.make_async_copy(a, b, wsem.at[k])
                 for k, (a, b) in enumerate(((vr_hbm, vr), (kr_hbm, kr), (rate_hbm, rate), (cnt_hbm, cnt)))]
        for c in small:
            c.start()

        def group(hbm, ref, g, sem, out=False):
            sl = pl.ds(pl.multiple_of(8 * g, 8), 8)
            a, b = hbm.at[:, sl, :], ref.at[g]
            return pltpu.make_async_copy(b, a, sem) if out else pltpu.make_async_copy(a, b, sem)

        for g in range(8):
            group(vib_hbm, vib, g, sems.at[0, g]).start()
            group(sp_hbm, sp, g, sems.at[1, g]).start()
        for c in small:
            c.wait()
        powers(vr, kr, va, sa, w_scr, w8_scr)
        v2 = vib.reshape(8 * 368, 128)
        s2 = sp.reshape(8 * 240, 128)
        vo2 = vo.reshape(8 * 368, 128)
        so2 = so.reshape(8 * 240, 128)

        for g in range(8):
            coefs(rate[8 * g : 8 * g + 8, :], group_counts(cnt, g), s_scr, 8 * g)

        def ready(g):
            group(vib_hbm, vib, g, sems.at[0, g]).wait()
            group(sp_hbm, sp, g, sems.at[1, g]).wait()

        def emit(g):
            group(vo_hbm, vo, g, osems.at[0, g], True).start()
            group(so_hbm, so, g, osems.at[1, g], True).start()

        def cf(g, k, j):
            at = 8 * g + 2 * k
            return jnp.concatenate([s_scr[j - 1, pl.ds(at, 1), :], s_scr[j - 1, pl.ds(at + 1, 1), :]], 1)

        def expand(g, k, slot):
            p_scr[slot] = jnp.dot(w_scr[...], split_stack(load_pair(v2, s2, g, k)), preferred_element_type=F32)

        def combine(g, k, slot):
            x = load_pair(v2, s2, g, k)
            y0 = x
            y1 = cf(g, k, 8) * x
            for j in range(1, 9):
                w = p_scr[slot, 80 * (j - 1) : 80 * j, :]
                if j < 8:
                    y0 = y0 + cf(g, k, j) * w
                y1 = y1 + cf(g, k, 8 + j) * w
            y_scr[slot] = y0
            y1_scr[slot] = jnp.concatenate([y1.astype(BF16), jnp.zeros((48, 256), BF16)], 0)

        def finish(g, k, slot):
            z = jnp.dot(w8_scr[...], y1_scr[slot], preferred_element_type=F32)
            out = cf(g, k, 17) * (y_scr[slot] + z)
            for h in range(2):
                part = out[:, 128 * h : 128 * h + 128]
                for m, o in enumerate(VO):
                    vo2[pl.ds(g * 368 + (o * 8 + 2 * k + h), 8, stride=8), :] = part[8 * m : 8 * m + 8, :]
                for m, o in enumerate(SO):
                    so2[pl.ds(g * 240 + (o * 8 + 2 * k + h), 8, stride=8), :] = part[48 + 8 * m : 56 + 8 * m, :]

        ready(0)
        expand(0, 0, 0)
        y_scr[1] = jnp.zeros((80, 256), F32)
        y1_scr[1] = jnp.zeros((128, 256), BF16)

        @pl.loop(0, 8)
        def _(g):
            pl.when(g < 7)(lambda: ready(g + 1))
            for k in range(4):
                expand(jnp.minimum(g + 1, 7) if k == 3 else g, (k + 1) % 4, (k + 1) % 2)
                finish(jnp.maximum(g - 1, 0) if k == 0 else g, (k - 1) % 4, (k + 1) % 2)
                combine(g, k, k % 2)
            pl.when(g > 0)(lambda: emit(g - 1))

        finish(7, 3, 1)
        emit(7)
        for g in range(8):
            group(vo_hbm, vo, g, osems.at[0, g], True).wait()
            group(so_hbm, so, g, osems.at[1, g], True).wait()


def chem(early, vib, sp, rate, cnt, vr, kr, extra):
    hbm = pl.BlockSpec(memory_space=pl.ANY)
    n = len(extra)
    like = lambda v: jax.ShapeDtypeStruct(v.shape, v.dtype)
    outs = [like(vib), like(sp)] + ([like(v) for v in extra] if early else [])
    out = pl.pallas_call(
        functools.partial(chem_kernel, early),
        in_specs=[hbm] * (6 + n),
        out_specs=[hbm] * len(outs),
        out_shape=outs,
        input_output_aliases={6 + k: k + (2 if early else 0) for k in range(n)},
        scratch_shapes=[pltpu.VMEM((46, 46), F32), pltpu.VMEM((30, 30), F32), pltpu.SMEM((64,), jnp.int32),
                        pltpu.VMEM((64, 128), F32)]
        + [pltpu.VMEM((8, k, 8, 128), F32) for k in (46, 30, 46, 30)]
        + [pltpu.VMEM((48, 128), F32), pltpu.VMEM((32, 128), F32),
           pltpu.VMEM((640, 256), BF16), pltpu.VMEM((80, 128), BF16),
           pltpu.VMEM((17, 64, 128), F32), pltpu.VMEM((2, 640, 256), F32),
           pltpu.VMEM((2, 80, 256), F32), pltpu.VMEM((2, 128, 256), BF16),
           pltpu.SemaphoreType.DMA((2, 8)), pltpu.SemaphoreType.DMA((2, 8)), pltpu.SemaphoreType.DMA((4,))],
        compiler_params=pltpu.CompilerParams(vmem_limit_bytes=62 * 2**20),
        cost_estimate=pl.CostEstimate(flops=10**9, bytes_accessed=6 * 10**6, transcendentals=0),
        name="chemistry_early" if early else "chemistry_late",
    )(vr, kr, cnt, rate, vib, sp, *extra)
    return out[:2], out[2:]


def cell_flux(q, d):
    inv = 1.0 / q[0]
    u = q[d] * inv
    p = 0.4 * (q[4] - 0.5 * (q[1] * q[1] + q[2] * q[2] + q[3] * q[3]) * inv)
    f = [q[d], q[1] * u, q[2] * u, q[3] * u, (q[4] + p) * u]
    f[d] = f[d] + p
    return f, jnp.abs(u) + jnp.sqrt(1.4 * p * inv)


def recip(v):
    return pl.reciprocal(v, approx=True)


def side(v2, d0, d1, d2, d3):
    c0, c1, c2 = d1 - d0, d2 - d1, d3 - d2
    t1 = 3.0 * d1
    e0 = t1 - d0
    e1 = d1 + d2
    e2 = d3 - 3.0 * d2
    k = 13.0 / 3.0
    s0 = 1.6e-5 + (k * (c0 * c0) + e0 * e0)
    s1 = 1.6e-5 + (k * (c1 * c1) + e1 * e1)
    s2 = 1.6e-5 + (k * (c2 * c2) + e2 * e2)
    r0, r1, r2 = recip(s0), recip(s1), recip(s2)
    a0 = r0 * r0
    a1 = 6.0 * (r1 * r1)
    a2 = 3.0 * (r2 * r2)
    num = a0 * ((c0 + c0) + t1) + a1 * (e1 + d2) + a2 * (d2 - e2)
    den = a0 + a1 + a2
    return v2 + num * recip(6.0 * den)


def face(f, q, alpha):
    fd = [f[k + 1] - f[k] for k in range(5)]
    qd = [alpha * (q[k + 1] - q[k]) for k in range(5)]
    plus = side(f[2] + alpha * q[2], *[fd[k] + qd[k] for k in range(4)])
    m = [qd[k] - fd[k] for k in range(5)]
    minus = side(f[3] - alpha * q[3], m[4], m[3], m[2], m[1])
    return plus + minus


def weno_kernel(flow_ref, e_ref, xb_ref, yb_ref, xa_ref, ya_ref, own_ref, out_ref, xq, xf, xs, xg):
    even_x = lax.axis_index("gx") % 2 == 0
    even_y = lax.axis_index("gy") % 2 == 0
    xa, xb, ya, yb = xa_ref[...], xb_ref[...], ya_ref[0:8, :], yb_ref[0:8, :]
    up, dn = jnp.where(even_x, xb, xa), jnp.where(even_x, xa, xb)
    lq, rq = jnp.where(even_y, yb, ya), jnp.where(even_y, ya, yb)
    for c in range(5):
        xq[c, 5:8, :] = up[3 * c : 3 * c + 3, :]
        xq[c, 8:72, :] = e_ref[...] if c == 4 else flow_ref[c]
        xq[c, 72:75, :] = dn[3 * c : 3 * c + 3, :]
    one = jnp.ones((5, 128), F32)
    for c in range(5):
        fill = one if c in (0, 4) else 0.0 * one
        xq[c, 0:5, :] = fill
        xq[c, 75:80, :] = fill
    for g in range(10):
        sl = slice(8 * g, 8 * g + 8)
        f, s = cell_flux([xq[c, sl, :] for c in range(5)], 1)
        for c in range(5):
            xf[c, sl, :] = f[c]
        xs[sl, :] = s
    for g in range(9):
        b = 8 * g + 5
        n = 8 if g < 8 else 1
        alpha = xs[b : b + n, :]
        for o in range(1, 6):
            alpha = jnp.maximum(alpha, xs[b + o : b + o + n, :])
        for c in range(5):
            xg[c, 8 * g : 8 * g + n, :] = face(
                [xf[c, b + o : b + o + n, :] for o in range(6)],
                [xq[c, b + o : b + o + n, :] for o in range(6)],
                alpha,
            )

    lane = lax.broadcasted_iota(jnp.int32, (8, 128), 1)
    slot = lane % 16

    def shift(v, k):
        return v if k % 128 == 0 else pltpu.roll(v, (-k) % 128, 1)

    def strip(v):
        q = [shift(v, 3 * c) for c in range(5)]
        f, s = cell_flux(q, 2)
        ff = f[0]
        ss = s
        for c in range(1, 5):
            here = slot >= 3 * c
            ff = jnp.where(here, shift(f[c], -3 * c), ff)
            ss = jnp.where(here, shift(s, -3 * c), ss)
        return v, ff, ss

    lq, lfx, ls = strip(lq)
    oq, ofx, os_ = strip(own_ref[...])
    alpha = ls
    for v in (shift(ls, 1), shift(ls, 2), os_, shift(os_, 1), shift(os_, 2)):
        alpha = jnp.maximum(alpha, v)
    first = face(
        [lfx, shift(lfx, 1), shift(lfx, 2), ofx, shift(ofx, 1), shift(ofx, 2)],
        [lq, shift(lq, 1), shift(lq, 2), oq, shift(oq, 1), shift(oq, 2)],
        alpha,
    )
    for g in range(8):
        sl = slice(8 * g + 8, 8 * g + 16)
        q = [xq[c, sl, :] for c in range(5)]
        h = [
            jnp.where(lane < 64, shift(rq, 16 * g + 3 * c), shift(lq, 16 * g + 3 * c - 125)) for c in range(5)
        ]
        f, s = cell_flux(q, 2)
        hf, hs = cell_flux(h, 2)

        def six(a, b):
            out = []
            for o in range(-2, 4):
                if o == 0:
                    out.append(a)
                elif o > 0:
                    out.append(shift(jnp.where(lane < o, b, a), o))
                else:
                    out.append(shift(jnp.where(lane >= 128 + o, b, a), o))
            return out

        alphas = six(s, hs)
        alpha = alphas[0]
        for v in alphas[1:]:
            alpha = jnp.maximum(alpha, v)
        qs = [six(q[c], h[c]) for c in range(5)]
        for c in range(5):
            after = face(qs[2] if c == 0 else six(f[c], hf[c]), qs[c], alpha)
            before = jnp.where(lane == 0, shift(first, 16 * g + 3 * c), shift(after, -1))
            gx = xg[c, 8 * g + 1 : 8 * g + 9, :] - xg[c, 8 * g : 8 * g + 8, :]
            out_ref[c, 8 * g : 8 * g + 8, :] = q[c] - 0.05 * (gx + (after - before))


def weno(flow, e, xb, yb, xa, ya, own):
    vm = pl.BlockSpec(memory_space=pltpu.VMEM)
    return pl.pallas_call(
        weno_kernel,
        in_specs=[vm] * 7,
        out_specs=vm,
        out_shape=jax.ShapeDtypeStruct((5, 64, 128), F32),
        scratch_shapes=[pltpu.VMEM((5, 80, 128), F32), pltpu.VMEM((5, 80, 128), F32), pltpu.VMEM((80, 128), F32),
                        pltpu.VMEM((5, 72, 128), F32)],
        compiler_params=pltpu.CompilerParams(vmem_limit_bytes=20 * 2**20),
        cost_estimate=pl.CostEstimate(flops=10**7, bytes_accessed=10**6, transcendentals=0),
        name="euler_weno",
    )(flow, e, xb, yb, xa, ya, own)


def swaps(size, start):
    pairs = [(i % size, (i + 1) % size) for i in range(start, size, 2)]
    return pairs + [(b, a) for a, b in pairs]


def swapped(value, axis, start):
    return lax.ppermute(value, axis, swaps(lax.axis_size(axis), start))


def local(flow, vib, species, field_rate, substeps, vib_rates, kin_rates, level_energy, formation_heat):
    counts = substeps.reshape(-1)
    e, xa, xb, ya, yb, own = heat(
        flow, vib, species, field_rate, counts, vib_rates, kin_rates, level_energy, formation_heat
    )
    first, (xa, xb, ya, yb) = chem(
        True, vib, species, field_rate, counts, vib_rates, kin_rates, (xa, xb, ya, yb)
    )
    xb = swapped(xb, "gx", 1)
    yb = swapped(yb, "gy", 1)
    xa = swapped(xa, "gx", 0)
    ya = swapped(ya, "gy", 0)
    (vib_final, species_final), _ = chem(False, vib, species, field_rate, counts, vib_rates, kin_rates, first)
    return (weno(flow, e, xb, yb, xa, ya, own), vib_final, species_final)


def solution(mesh):
    tiled = P(None, "gx", "gy")
    return jax.shard_map(
        local,
        mesh=mesh,
        in_specs=(tiled, tiled, tiled, P("gx", "gy"), P("gx", "gy"), P(), P(), P(), P()),
        out_specs=(tiled, tiled, tiled),
        check_vma=False,
    )
```

```python
import functools

import jax
import jax.numpy as jnp
from jax import lax
from jax.experimental import pallas as pl
from jax.experimental.pallas import tpu as pltpu
from jax.sharding import PartitionSpec as P

F32, BF16 = jnp.float32, jnp.bfloat16
HIGH = lax.Precision.HIGHEST
VO = (0, 8, 16, 24, 32, 38)
SO = (0, 8, 16, 22)


def widen_rates(vr_ref, kr_ref, va, sa):
    va[...] = jnp.zeros_like(va)
    sa[...] = jnp.zeros_like(sa)
    va[0:40, 0:46] = vr_ref[0:40, :]
    va[40:48, 0:46] = vr_ref[38:46, :]
    sa[0:24, 0:30] = kr_ref[0:24, :]
    sa[24:32, 0:30] = kr_ref[22:30, :]
    v = va[...]
    s = sa[...]
    lane = lax.broadcasted_iota(jnp.int32, (48, 128), 1)
    v = jnp.where(lane < 38, v, jnp.where((lane >= 40) & (lane < 48), pltpu.roll(v, 2, 1), 0.0))
    lane = lax.broadcasted_iota(jnp.int32, (32, 128), 1)
    s = jnp.where(
        (lane >= 48) & (lane < 70),
        pltpu.roll(s, 48, 1),
        jnp.where((lane >= 72) & (lane < 80), pltpu.roll(s, 50, 1), 0.0),
    )
    b = jnp.concatenate([v, s, jnp.zeros((48, 128), F32)], 0)
    row = lax.broadcasted_iota(jnp.int32, (128, 128), 0)
    col = lax.broadcasted_iota(jnp.int32, (128, 128), 1)
    rid = jnp.where(row < 40, row, jnp.where(row < 48, row - 2, jnp.where(row < 72, row + 52, row + 50)))
    cid = jnp.where(
        col < 38,
        col,
        jnp.where(
            (col >= 40) & (col < 48),
            col - 2,
            jnp.where((col >= 48) & (col < 70), col + 52, jnp.where((col >= 72) & (col < 80), col + 50, -1)),
        ),
    )
    return b + jnp.where((rid == cid) & (row < 80), 2.0, 0.0)


def pack_split(m):
    hi = m.astype(BF16).astype(F32)
    lo = m - hi
    lane = lax.broadcasted_iota(jnp.int32, m.shape, 1)
    first = jnp.where(lane < 80, hi, pltpu.roll(hi, 80, 1))
    second = jnp.where(lane < 32, pltpu.roll(hi, 80, 1), pltpu.roll(lo, 32, 1))
    return jnp.concatenate([first, second], 1).astype(BF16)


def mm(a, b):
    ah, bh = a.astype(BF16), b.astype(BF16)
    al, bl = (a - ah.astype(F32)).astype(BF16), (b - bh.astype(F32)).astype(BF16)
    out = jnp.dot(jnp.concatenate([ah, al], 1), jnp.concatenate([bh, bh], 0), preferred_element_type=F32)
    return out + jnp.dot(ah, bl, preferred_element_type=F32)


def load_pair(v2, s2, g, k):
    def one(r):
        return jnp.concatenate(
            [v2[pl.ds(g * 368 + (o * 8 + r), 8, stride=8), :] for o in VO]
            + [s2[pl.ds(g * 240 + (o * 8 + r), 8, stride=8), :] for o in SO], 0)

    return jnp.concatenate([one(2 * k), one(2 * k + 1)], 1)


def split_stack(x):
    hi = x.astype(BF16)
    lo = (x - hi.astype(F32)).astype(BF16)
    return jnp.concatenate([hi, lo, hi, jnp.zeros((16, 256), BF16)], 0)


def group_counts(cnt_ref, g):
    row = lax.broadcasted_iota(jnp.int32, (8, 128), 0)
    n = jnp.zeros((8, 128), jnp.int32)
    for r in range(8):
        n = jnp.where(row == r, cnt_ref[g * 8 + r], n)
    return n.astype(F32)


def heat_kernel(vr_hbm, kr_hbm, ev_hbm, es_hbm, cnt_hbm, rate_hbm, flow_hbm, vib_hbm, sp_hbm,
                e_ref, xa_ref, xb_ref, ya_ref, yb_ref, own_ref,
                vr_ref, kr_ref, ev_ref, es_ref, cnt_ref, rate_ref, flow_ref,
                vib, sp, va, sa, ee, g_scr, s_scr, p_scr, w_scr, sems, wsem):
    small = [pltpu.make_async_copy(a, b, wsem.at[k])
             for k, (a, b) in enumerate(((vr_hbm, vr_ref), (kr_hbm, kr_ref), (ev_hbm, ev_ref), (es_hbm, es_ref),
                                         (cnt_hbm, cnt_ref), (rate_hbm, rate_ref), (flow_hbm, flow_ref)))]
    for c in small[:6]:
        c.start()

    def pieces(g):
        sl = pl.ds(pl.multiple_of(8 * g, 8), 8)
        return (pltpu.make_async_copy(vib_hbm.at[:, sl, :], vib.at[g], sems.at[0, g]),
                pltpu.make_async_copy(sp_hbm.at[:, sl, :], sp.at[g], sems.at[1, g]))

    for g in range(8):
        for c in pieces(g):
            c.start()
    small[6].start()
    for c in small[:6]:
        c.wait()
    for g in range(8):
        coefs(rate_ref[8 * g : 8 * g + 8, :], group_counts(cnt_ref, g), s_scr, 8 * g)

    b1 = widen_rates(vr_ref, kr_ref, va, sa)
    ee[...] = jnp.zeros_like(ee)
    ee[0:1, 0:46] = ev_ref[...]
    ee[8:9, 0:30] = es_ref[...]
    lane = lax.broadcasted_iota(jnp.int32, (8, 128), 1)
    v, s = ee[0:8, :], ee[8:16, :]
    v = jnp.where(lane < 38, v, jnp.where((lane >= 40) & (lane < 48), pltpu.roll(v, 2, 1), 0.0))
    v = jnp.where((lane >= 48) & (lane < 70), pltpu.roll(s, 48, 1),
                  jnp.where((lane >= 72) & (lane < 80), pltpu.roll(s, 50, 1), v))
    G = jnp.concatenate([v, jnp.zeros((24, 128), F32)], 0)
    b2 = mm(b1, b1)
    G = G + pltpu.roll(mm(G, b1), 1, 0)
    b4 = mm(b2, b2)
    G = G + pltpu.roll(mm(G, b2), 2, 0)
    b8 = mm(b4, b4)
    G = G + pltpu.roll(mm(G, b4), 4, 0)
    G = G + pltpu.roll(mm(G, b8), 8, 0)
    row = lax.broadcasted_iota(jnp.int32, (32, 128), 0)
    G = G + jnp.where(row == 16, pltpu.roll(mm(G, b8), 8, 0), 0.0)
    g_scr[...] = pack_split(G)

    v2 = vib.reshape(8 * 368, 128)
    s2 = sp.reshape(8 * 240, 128)
    even_x = lax.axis_index("gx") % 2 == 0
    even_y = lax.axis_index("gy") % 2 == 0
    small[6].wait()

    def sums(g, left, right):
        sl = pl.ds(pl.multiple_of(8 * g, 8), 8)
        first = p_scr[pl.ds(192 * g, 8, stride=24), :]
        acc = first
        for j in range(1, 17):
            acc = acc + s_scr[j - 1, sl, :] * p_scr[pl.ds(192 * g + j, 8, stride=24), :]
        e = flow_ref[4, sl, :] + (first - s_scr[16, sl, :] * acc)
        e_ref[sl, :] = e
        for c in range(5):
            at = 16 * g + 3 * c
            v = e if c == 4 else flow_ref[c, sl, :]
            here = (lane >= at) & (lane < at + 3)
            left = jnp.where(here, pltpu.roll(v, at, 1), left)
            right = jnp.where(here, pltpu.roll(v, lax.rem(at + 3, 128), 1), right)
        return left, right

    p_scr[0:192, :] = jnp.zeros((192, 128), F32)

    def turn(g, carry):
        for c in pieces(g):
            c.wait()
        for i in range(4):
            r = 8 * g + 2 * i
            w = jnp.dot(g_scr[...], split_stack(load_pair(v2, s2, g, i)), preferred_element_type=F32)
            w_scr[48 * i : 48 * i + 24, :] = w[0:24, 0:128]
            w_scr[48 * i + 24 : 48 * i + 48, :] = w[0:24, 128:256]
        out = sums(jnp.maximum(g - 1, 0), *carry)
        p_scr[pl.ds(pl.multiple_of(192 * g, 8), 192), :] = w_scr[...]
        return out

    left = jnp.ones((8, 128), F32)
    left, right = lax.fori_loop(0, 8, turn, (left, left), unroll=4)
    left, right = sums(7, left, right)
    edge = {}
    for g in (0, 7):
        sl = slice(8 * g, 8 * g + 8)
        edge[g] = [flow_ref[c, sl, :] for c in range(4)] + [e_ref[sl, :]]
    own_ref[...] = left
    ya_ref[0:8, :] = jnp.where(even_y, right, left)
    yb_ref[0:8, :] = jnp.where(even_y, left, right)
    ya_ref[8:16, :] = jnp.ones((8, 128), F32)
    yb_ref[8:16, :] = jnp.ones((8, 128), F32)
    for c in range(5):
        top, bottom = edge[0][c][0:3, :], edge[7][c][5:8, :]
        xa_ref[3 * c : 3 * c + 3, :] = jnp.where(even_x, bottom, top)
        xb_ref[3 * c : 3 * c + 3, :] = jnp.where(even_x, top, bottom)
    xa_ref[15:16, :] = jnp.ones((1, 128), F32)
    xb_ref[15:16, :] = jnp.ones((1, 128), F32)


def heat(flow, vib, sp, rate, cnt, vr, kr, ev, es):
    vm = pl.BlockSpec(memory_space=pltpu.VMEM)
    hbm = pl.BlockSpec(memory_space=pl.ANY)
    return pl.pallas_call(
        heat_kernel,
        in_specs=[hbm] * 9,
        out_specs=[vm] * 6,
        out_shape=[jax.ShapeDtypeStruct((k, 128), F32) for k in (64, 16, 16, 16, 16, 8)],
        scratch_shapes=[pltpu.VMEM((46, 46), F32), pltpu.VMEM((30, 30), F32), pltpu.VMEM((1, 46), F32),
                        pltpu.VMEM((1, 30), F32), pltpu.SMEM((64,), jnp.int32), pltpu.VMEM((64, 128), F32),
                        pltpu.VMEM((5, 64, 128), F32),
                        pltpu.VMEM((8, 46, 8, 128), F32), pltpu.VMEM((8, 30, 8, 128), F32),
                        pltpu.VMEM((48, 128), F32), pltpu.VMEM((32, 128), F32), pltpu.VMEM((16, 128), F32),
                        pltpu.VMEM((32, 256), BF16), pltpu.VMEM((17, 64, 128), F32), pltpu.VMEM((1536, 128), F32),
                        pltpu.VMEM((192, 128), F32),
                        pltpu.SemaphoreType.DMA((2, 8)), pltpu.SemaphoreType.DMA((7,))],
        compiler_params=pltpu.CompilerParams(vmem_limit_bytes=62 * 2**20),
        cost_estimate=pl.CostEstimate(flops=10**8, bytes_accessed=3 * 10**6, transcendentals=0),
        name="heat",
    )(vr, kr, ev.reshape(1, -1), es.reshape(1, -1), cnt, rate, flow, vib, sp)


def powers(vr_ref, kr_ref, va, sa, w_scr, w8_scr):
    b1 = widen_rates(vr_ref, kr_ref, va, sa)
    b2 = mm(b1, b1)
    b3 = mm(b2, b1)
    b4 = mm(b2, b2)
    b5 = mm(b4, b1)
    b6 = mm(b4, b2)
    b7 = mm(b4, b3)
    b8 = mm(b4, b4)
    for j, m in enumerate((b1, b2, b3, b4, b5, b6, b7, b8)):
        w_scr[80 * j : 80 * j + 80, :] = pack_split(m[0:80])
    w8_scr[...] = b8[0:80].astype(BF16)


def coefs(rate, n, s_scr, at):
    hr = 0.05 * rate
    a = 1.0 - 2.0 * hr
    t = hr / a
    s = n * t
    s_scr[0, at : at + 8, :] = s
    for j in range(1, 16):
        s = s * (((n - j) * (1.0 / (j + 1))) * t)
        s_scr[j, at : at + 8, :] = s
    m = n.astype(jnp.int32)
    p = jnp.ones_like(a)
    q = a
    for k in range(5):
        p = jnp.where(((m >> k) & 1) == 1, p * q, p)
        if k < 4:
            q = q * q
    s_scr[16, at : at + 8, :] = p


def chem_kernel(early, vr_hbm, kr_hbm, cnt_hbm, rate_hbm, vib_hbm, sp_hbm, *rest):
    vo_hbm, so_hbm = rest[4:6] if early else rest[2:4]
    vr, kr, cnt, rate, vib, sp, vo, so, va, sa, w_scr, w8_scr, s_scr, p_scr, y_scr, y1_scr, sems, osems, wsem = rest[-19:]
    half = lax.axis_size("gx") // 2

    @pl.when(((lax.axis_index("gx") < half) & (lax.axis_index("gy") % 8 < 4)) == early)
    def _():
        small = [pltpu.make_async_copy(a, b, wsem.at[k])
                 for k, (a, b) in enumerate(((vr_hbm, vr), (kr_hbm, kr), (rate_hbm, rate), (cnt_hbm, cnt)))]
        for c in small:
            c.start()

        def group(hbm, ref, g, sem, out=False):
            sl = pl.ds(pl.multiple_of(8 * g, 8), 8)
            a, b = hbm.at[:, sl, :], ref.at[g]
            return pltpu.make_async_copy(b, a, sem) if out else pltpu.make_async_copy(a, b, sem)

        for g in range(8):
            group(vib_hbm, vib, g, sems.at[0, g]).start()
            group(sp_hbm, sp, g, sems.at[1, g]).start()
        for c in small:
            c.wait()
        powers(vr, kr, va, sa, w_scr, w8_scr)
        v2 = vib.reshape(8 * 368, 128)
        s2 = sp.reshape(8 * 240, 128)
        vo2 = vo.reshape(8 * 368, 128)
        so2 = so.reshape(8 * 240, 128)

        for g in range(8):
            coefs(rate[8 * g : 8 * g + 8, :], group_counts(cnt, g), s_scr, 8 * g)

        def ready(g):
            group(vib_hbm, vib, g, sems.at[0, g]).wait()
            group(sp_hbm, sp, g, sems.at[1, g]).wait()

        def emit(g):
            group(vo_hbm, vo, g, osems.at[0, g], True).start()
            group(so_hbm, so, g, osems.at[1, g], True).start()

        def cf(g, k, j):
            at = 8 * g + 2 * k
            return jnp.concatenate([s_scr[j - 1, pl.ds(at, 1), :], s_scr[j - 1, pl.ds(at + 1, 1), :]], 1)

        def expand(g, k, slot):
            p_scr[slot] = jnp.dot(w_scr[...], split_stack(load_pair(v2, s2, g, k)), preferred_element_type=F32)

        def combine(g, k, slot):
            x = load_pair(v2, s2, g, k)
            y0 = x
            y1 = cf(g, k, 8) * x
            for j in range(1, 9):
                w = p_scr[slot, 80 * (j - 1) : 80 * j, :]
                if j < 8:
                    y0 = y0 + cf(g, k, j) * w
                y1 = y1 + cf(g, k, 8 + j) * w
            y_scr[slot] = y0
            y1_scr[slot] = jnp.concatenate([y1.astype(BF16), jnp.zeros((48, 256), BF16)], 0)

        def finish(g, k, slot):
            z = jnp.dot(w8_scr[...], y1_scr[slot], preferred_element_type=F32)
            out = cf(g, k, 17) * (y_scr[slot] + z)
            for h in range(2):
                part = out[:, 128 * h : 128 * h + 128]
                for m, o in enumerate(VO):
                    vo2[pl.ds(g * 368 + (o * 8 + 2 * k + h), 8, stride=8), :] = part[8 * m : 8 * m + 8, :]
                for m, o in enumerate(SO):
                    so2[pl.ds(g * 240 + (o * 8 + 2 * k + h), 8, stride=8), :] = part[48 + 8 * m : 56 + 8 * m, :]

        ready(0)
        expand(0, 0, 0)
        y_scr[1] = jnp.zeros((80, 256), F32)
        y1_scr[1] = jnp.zeros((128, 256), BF16)

        @pl.loop(0, 8)
        def _(g):
            pl.when(g < 7)(lambda: ready(g + 1))
            for k in range(4):
                expand(jnp.minimum(g + 1, 7) if k == 3 else g, (k + 1) % 4, (k + 1) % 2)
                finish(jnp.maximum(g - 1, 0) if k == 0 else g, (k - 1) % 4, (k + 1) % 2)
                combine(g, k, k % 2)
            pl.when(g > 0)(lambda: emit(g - 1))

        finish(7, 3, 1)
        emit(7)
        for g in range(8):
            group(vo_hbm, vo, g, osems.at[0, g], True).wait()
            group(so_hbm, so, g, osems.at[1, g], True).wait()


def chem(early, vib, sp, rate, cnt, vr, kr, extra):
    hbm = pl.BlockSpec(memory_space=pl.ANY)
    n = len(extra)
    like = lambda v: jax.ShapeDtypeStruct(v.shape, v.dtype)
    outs = [like(vib), like(sp)] + ([like(v) for v in extra] if early else [])
    out = pl.pallas_call(
        functools.partial(chem_kernel, early),
        in_specs=[hbm] * (6 + n),
        out_specs=[hbm] * len(outs),
        out_shape=outs,
        input_output_aliases={6 + k: k + (2 if early else 0) for k in range(n)},
        scratch_shapes=[pltpu.VMEM((46, 46), F32), pltpu.VMEM((30, 30), F32), pltpu.SMEM((64,), jnp.int32),
                        pltpu.VMEM((64, 128), F32)]
        + [pltpu.VMEM((8, k, 8, 128), F32) for k in (46, 30, 46, 30)]
        + [pltpu.VMEM((48, 128), F32), pltpu.VMEM((32, 128), F32),
           pltpu.VMEM((640, 256), BF16), pltpu.VMEM((80, 128), BF16),
           pltpu.VMEM((17, 64, 128), F32), pltpu.VMEM((2, 640, 256), F32),
           pltpu.VMEM((2, 80, 256), F32), pltpu.VMEM((2, 128, 256), BF16),
           pltpu.SemaphoreType.DMA((2, 8)), pltpu.SemaphoreType.DMA((2, 8)), pltpu.SemaphoreType.DMA((4,))],
        compiler_params=pltpu.CompilerParams(vmem_limit_bytes=62 * 2**20),
        cost_estimate=pl.CostEstimate(flops=10**9, bytes_accessed=6 * 10**6, transcendentals=0),
        name="chemistry_early" if early else "chemistry_late",
    )(vr, kr, cnt, rate, vib, sp, *extra)
    return out[:2], out[2:]


def cell_flux(q, d):
    inv = 1.0 / q[0]
    u = q[d] * inv
    p = 0.4 * (q[4] - 0.5 * (q[1] * q[1] + q[2] * q[2] + q[3] * q[3]) * inv)
    f = [q[d], q[1] * u, q[2] * u, q[3] * u, (q[4] + p) * u]
    f[d] = f[d] + p
    return f, jnp.abs(u) + jnp.sqrt(1.4 * p * inv)


def recip(v):
    return pl.reciprocal(v, approx=True)


def side(v2, d0, d1, d2, d3):
    c0, c1, c2 = d1 - d0, d2 - d1, d3 - d2
    t1 = 3.0 * d1
    e0 = t1 - d0
    e1 = d1 + d2
    e2 = d3 - 3.0 * d2
    k = 13.0 / 3.0
    s0 = 1.6e-5 + (k * (c0 * c0) + e0 * e0)
    s1 = 1.6e-5 + (k * (c1 * c1) + e1 * e1)
    s2 = 1.6e-5 + (k * (c2 * c2) + e2 * e2)
    r0, r1, r2 = recip(s0), recip(s1), recip(s2)
    a0 = r0 * r0
    a1 = 6.0 * (r1 * r1)
    a2 = 3.0 * (r2 * r2)
    num = a0 * ((c0 + c0) + t1) + a1 * (e1 + d2) + a2 * (d2 - e2)
    den = a0 + a1 + a2
    return v2 + num * recip(6.0 * den)


def face(f, q, alpha):
    fd = [f[k + 1] - f[k] for k in range(5)]
    qd = [alpha * (q[k + 1] - q[k]) for k in range(5)]
    plus = side(f[2] + alpha * q[2], *[fd[k] + qd[k] for k in range(4)])
    m = [qd[k] - fd[k] for k in range(5)]
    minus = side(f[3] - alpha * q[3], m[4], m[3], m[2], m[1])
    return plus + minus


def weno_kernel(flow_ref, e_ref, xb_ref, yb_ref, xa_ref, ya_ref, own_ref, out_ref, xq, xf, xs, xg):
    even_x = lax.axis_index("gx") % 2 == 0
    even_y = lax.axis_index("gy") % 2 == 0
    xa, xb, ya, yb = xa_ref[...], xb_ref[...], ya_ref[0:8, :], yb_ref[0:8, :]
    up, dn = jnp.where(even_x, xb, xa), jnp.where(even_x, xa, xb)
    lq, rq = jnp.where(even_y, yb, ya), jnp.where(even_y, ya, yb)
    for c in range(5):
        xq[c, 5:8, :] = up[3 * c : 3 * c + 3, :]
        xq[c, 8:72, :] = e_ref[...] if c == 4 else flow_ref[c]
        xq[c, 72:75, :] = dn[3 * c : 3 * c + 3, :]
    one = jnp.ones((5, 128), F32)
    for c in range(5):
        fill = one if c in (0, 4) else 0.0 * one
        xq[c, 0:5, :] = fill
        xq[c, 75:80, :] = fill
    for g in range(10):
        sl = slice(8 * g, 8 * g + 8)
        f, s = cell_flux([xq[c, sl, :] for c in range(5)], 1)
        for c in range(5):
            xf[c, sl, :] = f[c]
        xs[sl, :] = s
    for g in range(9):
        b = 8 * g + 5
        n = 8 if g < 8 else 1
        alpha = xs[b : b + n, :]
        for o in range(1, 6):
            alpha = jnp.maximum(alpha, xs[b + o : b + o + n, :])
        for c in range(5):
            xg[c, 8 * g : 8 * g + n, :] = face(
                [xf[c, b + o : b + o + n, :] for o in range(6)],
                [xq[c, b + o : b + o + n, :] for o in range(6)],
                alpha,
            )

    lane = lax.broadcasted_iota(jnp.int32, (8, 128), 1)
    slot = lane % 16

    def shift(v, k):
        return v if k % 128 == 0 else pltpu.roll(v, (-k) % 128, 1)

    def strip(v):
        q = [shift(v, 3 * c) for c in range(5)]
        f, s = cell_flux(q, 2)
        ff = f[0]
        ss = s
        for c in range(1, 5):
            here = slot >= 3 * c
            ff = jnp.where(here, shift(f[c], -3 * c), ff)
            ss = jnp.where(here, shift(s, -3 * c), ss)
        return v, ff, ss

    lq, lfx, ls = strip(lq)
    oq, ofx, os_ = strip(own_ref[...])
    alpha = ls
    for v in (shift(ls, 1), shift(ls, 2), os_, shift(os_, 1), shift(os_, 2)):
        alpha = jnp.maximum(alpha, v)
    first = face(
        [lfx, shift(lfx, 1), shift(lfx, 2), ofx, shift(ofx, 1), shift(ofx, 2)],
        [lq, shift(lq, 1), shift(lq, 2), oq, shift(oq, 1), shift(oq, 2)],
        alpha,
    )
    for g in range(8):
        sl = slice(8 * g + 8, 8 * g + 16)
        q = [xq[c, sl, :] for c in range(5)]
        h = [
            jnp.where(lane < 64, shift(rq, 16 * g + 3 * c), shift(lq, 16 * g + 3 * c - 125)) for c in range(5)
        ]
        f, s = cell_flux(q, 2)
        hf, hs = cell_flux(h, 2)

        def six(a, b):
            out = []
            for o in range(-2, 4):
                if o == 0:
                    out.append(a)
                elif o > 0:
                    out.append(shift(jnp.where(lane < o, b, a), o))
                else:
                    out.append(shift(jnp.where(lane >= 128 + o, b, a), o))
            return out

        alphas = six(s, hs)
        alpha = alphas[0]
        for v in alphas[1:]:
            alpha = jnp.maximum(alpha, v)
        qs = [six(q[c], h[c]) for c in range(5)]
        for c in range(5):
            after = face(qs[2] if c == 0 else six(f[c], hf[c]), qs[c], alpha)
            before = jnp.where(lane == 0, shift(first, 16 * g + 3 * c), shift(after, -1))
            gx = xg[c, 8 * g + 1 : 8 * g + 9, :] - xg[c, 8 * g : 8 * g + 8, :]
            out_ref[c, 8 * g : 8 * g + 8, :] = q[c] - 0.05 * (gx + (after - before))


def weno(flow, e, xb, yb, xa, ya, own):
    vm = pl.BlockSpec(memory_space=pltpu.VMEM)
    return pl.pallas_call(
        weno_kernel,
        in_specs=[vm] * 7,
        out_specs=vm,
        out_shape=jax.ShapeDtypeStruct((5, 64, 128), F32),
        scratch_shapes=[pltpu.VMEM((5, 80, 128), F32), pltpu.VMEM((5, 80, 128), F32), pltpu.VMEM((80, 128), F32),
                        pltpu.VMEM((5, 72, 128), F32)],
        compiler_params=pltpu.CompilerParams(vmem_limit_bytes=20 * 2**20),
        cost_estimate=pl.CostEstimate(flops=10**7, bytes_accessed=10**6, transcendentals=0),
        name="euler_weno",
    )(flow, e, xb, yb, xa, ya, own)


def swaps(size, start):
    pairs = [(i % size, (i + 1) % size) for i in range(start, size, 2)]
    return pairs + [(b, a) for a, b in pairs]


def swapped(value, axis, start):
    return lax.ppermute(value, axis, swaps(lax.axis_size(axis), start))


def local(flow, vib, species, field_rate, substeps, vib_rates, kin_rates, level_energy, formation_heat):
    counts = substeps.reshape(-1)
    e, xa, xb, ya, yb, own = heat(
        flow, vib, species, field_rate, counts, vib_rates, kin_rates, level_energy, formation_heat
    )
    first, (xa, xb, ya, yb) = chem(
        True, vib, species, field_rate, counts, vib_rates, kin_rates, (xa, xb, ya, yb)
    )
    xb = swapped(xb, "gx", 1)
    yb = swapped(yb, "gy", 1)
    xa = swapped(xa, "gx", 0)
    ya = swapped(ya, "gy", 0)
    (vib_final, species_final), _ = chem(False, vib, species, field_rate, counts, vib_rates, kin_rates, first)
    return (weno(flow, e, xb, yb, xa, ya, own), vib_final, species_final)


def solution(mesh):
    tiled = P(None, "gx", "gy")
    return jax.shard_map(
        local,
        mesh=mesh,
        in_specs=(tiled, tiled, tiled, P("gx", "gy"), P("gx", "gy"), P(), P(), P(), P()),
        out_specs=(tiled, tiled, tiled),
        check_vma=False,
    )
```

```python
import functools

import jax
import jax.numpy as jnp
from jax import lax
from jax.experimental import pallas as pl
from jax.experimental.pallas import tpu as pltpu
from jax.sharding import PartitionSpec as P

F32, BF16 = jnp.float32, jnp.bfloat16
HIGH = lax.Precision.HIGHEST
VO = (0, 8, 16, 24, 32, 38)
SO = (0, 8, 16, 22)


def widen_rates(vr_ref, kr_ref, va, sa):
    va[...] = jnp.zeros_like(va)
    sa[...] = jnp.zeros_like(sa)
    va[0:40, 0:46] = vr_ref[0:40, :]
    va[40:48, 0:46] = vr_ref[38:46, :]
    sa[0:24, 0:30] = kr_ref[0:24, :]
    sa[24:32, 0:30] = kr_ref[22:30, :]
    v = va[...]
    s = sa[...]
    lane = lax.broadcasted_iota(jnp.int32, (48, 128), 1)
    v = jnp.where(lane < 38, v, jnp.where((lane >= 40) & (lane < 48), pltpu.roll(v, 2, 1), 0.0))
    lane = lax.broadcasted_iota(jnp.int32, (32, 128), 1)
    s = jnp.where(
        (lane >= 48) & (lane < 70),
        pltpu.roll(s, 48, 1),
        jnp.where((lane >= 72) & (lane < 80), pltpu.roll(s, 50, 1), 0.0),
    )
    b = jnp.concatenate([v, s, jnp.zeros((48, 128), F32)], 0)
    row = lax.broadcasted_iota(jnp.int32, (128, 128), 0)
    col = lax.broadcasted_iota(jnp.int32, (128, 128), 1)
    rid = jnp.where(row < 40, row, jnp.where(row < 48, row - 2, jnp.where(row < 72, row + 52, row + 50)))
    cid = jnp.where(
        col < 38,
        col,
        jnp.where(
            (col >= 40) & (col < 48),
            col - 2,
            jnp.where((col >= 48) & (col < 70), col + 52, jnp.where((col >= 72) & (col < 80), col + 50, -1)),
        ),
    )
    return b + jnp.where((rid == cid) & (row < 80), 2.0, 0.0)


def pack_split(m):
    hi = m.astype(BF16).astype(F32)
    lo = m - hi
    lane = lax.broadcasted_iota(jnp.int32, m.shape, 1)
    first = jnp.where(lane < 80, hi, pltpu.roll(hi, 80, 1))
    second = jnp.where(lane < 32, pltpu.roll(hi, 80, 1), pltpu.roll(lo, 32, 1))
    return jnp.concatenate([first, second], 1).astype(BF16)


def mm(a, b):
    ah, bh = a.astype(BF16), b.astype(BF16)
    al, bl = (a - ah.astype(F32)).astype(BF16), (b - bh.astype(F32)).astype(BF16)
    out = jnp.dot(jnp.concatenate([ah, al], 1), jnp.concatenate([bh, bh], 0), preferred_element_type=F32)
    return out + jnp.dot(ah, bl, preferred_element_type=F32)


def load_pair(v2, s2, g, k):
    def one(r):
        return jnp.concatenate(
            [v2[pl.ds(g * 368 + (o * 8 + r), 8, stride=8), :] for o in VO]
            + [s2[pl.ds(g * 240 + (o * 8 + r), 8, stride=8), :] for o in SO], 0)

    return jnp.concatenate([one(2 * k), one(2 * k + 1)], 1)


def split_stack(x):
    hi = x.astype(BF16)
    lo = (x - hi.astype(F32)).astype(BF16)
    return jnp.concatenate([hi, lo, hi, jnp.zeros((16, 256), BF16)], 0)


def group_counts(cnt_ref, g):
    row = lax.broadcasted_iota(jnp.int32, (8, 128), 0)
    n = jnp.zeros((8, 128), jnp.int32)
    for r in range(8):
        n = jnp.where(row == r, cnt_ref[g * 8 + r], n)
    return n.astype(F32)


def heat_kernel(vr_hbm, kr_hbm, ev_hbm, es_hbm, cnt_hbm, rate_hbm, flow_hbm, vib_hbm, sp_hbm,
                e_ref, xa_ref, xb_ref, ya_ref, yb_ref, own_ref,
                vr_ref, kr_ref, ev_ref, es_ref, cnt_ref, rate_ref, flow_ref,
                vib, sp, va, sa, ee, g_scr, s_scr, p_scr, w_scr, sems, wsem):
    small = [pltpu.make_async_copy(a, b, wsem.at[k])
             for k, (a, b) in enumerate(((vr_hbm, vr_ref), (kr_hbm, kr_ref), (ev_hbm, ev_ref), (es_hbm, es_ref),
                                         (cnt_hbm, cnt_ref), (rate_hbm, rate_ref), (flow_hbm, flow_ref)))]
    for c in small[:6]:
        c.start()

    def pieces(g):
        sl = pl.ds(pl.multiple_of(8 * g, 8), 8)
        return (pltpu.make_async_copy(vib_hbm.at[:, sl, :], vib.at[g], sems.at[0, g]),
                pltpu.make_async_copy(sp_hbm.at[:, sl, :], sp.at[g], sems.at[1, g]))

    for g in range(8):
        for c in pieces(g):
            c.start()
    small[6].start()
    for c in small[:6]:
        c.wait()
    for g in range(8):
        coefs(rate_ref[8 * g : 8 * g + 8, :], group_counts(cnt_ref, g), s_scr, 8 * g)

    b1 = widen_rates(vr_ref, kr_ref, va, sa)
    ee[...] = jnp.zeros_like(ee)
    ee[0:1, 0:46] = ev_ref[...]
    ee[8:9, 0:30] = es_ref[...]
    lane = lax.broadcasted_iota(jnp.int32, (8, 128), 1)
    v, s = ee[0:8, :], ee[8:16, :]
    v = jnp.where(lane < 38, v, jnp.where((lane >= 40) & (lane < 48), pltpu.roll(v, 2, 1), 0.0))
    v = jnp.where((lane >= 48) & (lane < 70), pltpu.roll(s, 48, 1),
                  jnp.where((lane >= 72) & (lane < 80), pltpu.roll(s, 50, 1), v))
    G = jnp.concatenate([v, jnp.zeros((24, 128), F32)], 0)
    b2 = mm(b1, b1)
    G = G + pltpu.roll(mm(G, b1), 1, 0)
    b4 = mm(b2, b2)
    G = G + pltpu.roll(mm(G, b2), 2, 0)
    b8 = mm(b4, b4)
    G = G + pltpu.roll(mm(G, b4), 4, 0)
    G = G + pltpu.roll(mm(G, b8), 8, 0)
    row = lax.broadcasted_iota(jnp.int32, (32, 128), 0)
    G = G + jnp.where(row == 16, pltpu.roll(mm(G, b8), 8, 0), 0.0)
    g_scr[...] = pack_split(G)

    v2 = vib.reshape(8 * 368, 128)
    s2 = sp.reshape(8 * 240, 128)
    even_x = lax.axis_index("gx") % 2 == 0
    even_y = lax.axis_index("gy") % 2 == 0
    small[6].wait()

    def sums(g, left, right):
        sl = pl.ds(pl.multiple_of(8 * g, 8), 8)
        first = p_scr[pl.ds(192 * g, 8, stride=24), :]
        acc = first
        for j in range(1, 17):
            acc = acc + s_scr[j - 1, sl, :] * p_scr[pl.ds(192 * g + j, 8, stride=24), :]
        e = flow_ref[4, sl, :] + (first - s_scr[16, sl, :] * acc)
        e_ref[sl, :] = e
        for c in range(5):
            at = 16 * g + 3 * c
            v = e if c == 4 else flow_ref[c, sl, :]
            here = (lane >= at) & (lane < at + 3)
            left = jnp.where(here, pltpu.roll(v, at, 1), left)
            right = jnp.where(here, pltpu.roll(v, lax.rem(at + 3, 128), 1), right)
        return left, right

    p_scr[0:192, :] = jnp.zeros((192, 128), F32)

    def turn(g, carry):
        for c in pieces(g):
            c.wait()
        for i in range(4):
            r = 8 * g + 2 * i
            w = jnp.dot(g_scr[...], split_stack(load_pair(v2, s2, g, i)), preferred_element_type=F32)
            w_scr[48 * i : 48 * i + 24, :] = w[0:24, 0:128]
            w_scr[48 * i + 24 : 48 * i + 48, :] = w[0:24, 128:256]
        out = sums(jnp.maximum(g - 1, 0), *carry)
        p_scr[pl.ds(pl.multiple_of(192 * g, 8), 192), :] = w_scr[...]
        return out

    left = jnp.ones((8, 128), F32)
    left, right = lax.fori_loop(0, 8, turn, (left, left), unroll=4)
    left, right = sums(7, left, right)
    edge = {}
    for g in (0, 7):
        sl = slice(8 * g, 8 * g + 8)
        edge[g] = [flow_ref[c, sl, :] for c in range(4)] + [e_ref[sl, :]]
    own_ref[...] = left
    ya_ref[0:8, :] = jnp.where(even_y, right, left)
    yb_ref[0:8, :] = jnp.where(even_y, left, right)
    ya_ref[8:16, :] = jnp.ones((8, 128), F32)
    yb_ref[8:16, :] = jnp.ones((8, 128), F32)
    for c in range(5):
        top, bottom = edge[0][c][0:3, :], edge[7][c][5:8, :]
        xa_ref[3 * c : 3 * c + 3, :] = jnp.where(even_x, bottom, top)
        xb_ref[3 * c : 3 * c + 3, :] = jnp.where(even_x, top, bottom)
    xa_ref[15:16, :] = jnp.ones((1, 128), F32)
    xb_ref[15:16, :] = jnp.ones((1, 128), F32)


def heat(flow, vib, sp, rate, cnt, vr, kr, ev, es):
    vm = pl.BlockSpec(memory_space=pltpu.VMEM)
    hbm = pl.BlockSpec(memory_space=pl.ANY)
    return pl.pallas_call(
        heat_kernel,
        in_specs=[hbm] * 9,
        out_specs=[vm] * 6,
        out_shape=[jax.ShapeDtypeStruct((k, 128), F32) for k in (64, 16, 16, 16, 16, 8)],
        scratch_shapes=[pltpu.VMEM((46, 46), F32), pltpu.VMEM((30, 30), F32), pltpu.VMEM((1, 46), F32),
                        pltpu.VMEM((1, 30), F32), pltpu.SMEM((64,), jnp.int32), pltpu.VMEM((64, 128), F32),
                        pltpu.VMEM((5, 64, 128), F32),
                        pltpu.VMEM((8, 46, 8, 128), F32), pltpu.VMEM((8, 30, 8, 128), F32),
                        pltpu.VMEM((48, 128), F32), pltpu.VMEM((32, 128), F32), pltpu.VMEM((16, 128), F32),
                        pltpu.VMEM((32, 256), BF16), pltpu.VMEM((17, 64, 128), F32), pltpu.VMEM((1536, 128), F32),
                        pltpu.VMEM((192, 128), F32),
                        pltpu.SemaphoreType.DMA((2, 8)), pltpu.SemaphoreType.DMA((7,))],
        compiler_params=pltpu.CompilerParams(vmem_limit_bytes=62 * 2**20),
        cost_estimate=pl.CostEstimate(flops=10**8, bytes_accessed=3 * 10**6, transcendentals=0),
        name="heat",
    )(vr, kr, ev.reshape(1, -1), es.reshape(1, -1), cnt, rate, flow, vib, sp)


def powers(vr_ref, kr_ref, va, sa, w_scr, w8_scr):
    b1 = widen_rates(vr_ref, kr_ref, va, sa)
    b2 = mm(b1, b1)
    b3 = mm(b2, b1)
    b4 = mm(b2, b2)
    b5 = mm(b4, b1)
    b6 = mm(b4, b2)
    b7 = mm(b4, b3)
    b8 = mm(b4, b4)
    for j, m in enumerate((b1, b2, b3, b4, b5, b6, b7, b8)):
        w_scr[80 * j : 80 * j + 80, :] = pack_split(m[0:80])
    w8_scr[...] = b8[0:80].astype(BF16)


def coefs(rate, n, s_scr, at):
    hr = 0.05 * rate
    a = 1.0 - 2.0 * hr
    t = hr / a
    s = n * t
    s_scr[0, at : at + 8, :] = s
    for j in range(1, 16):
        s = s * (((n - j) * (1.0 / (j + 1))) * t)
        s_scr[j, at : at + 8, :] = s
    m = n.astype(jnp.int32)
    p = jnp.ones_like(a)
    q = a
    for k in range(5):
        p = jnp.where(((m >> k) & 1) == 1, p * q, p)
        if k < 4:
            q = q * q
    s_scr[16, at : at + 8, :] = p


def chem_kernel(early, vr_hbm, kr_hbm, cnt_hbm, rate_hbm, vib_hbm, sp_hbm, *rest):
    vo_hbm, so_hbm = rest[4:6] if early else rest[2:4]
    vr, kr, cnt, rate, vib, sp, vo, so, va, sa, w_scr, w8_scr, s_scr, p_scr, y_scr, y1_scr, sems, osems, wsem = rest[-19:]
    half = lax.axis_size("gx") // 2

    @pl.when(((lax.axis_index("gx") < half) & (lax.axis_index("gy") % 8 < 4)) == early)
    def _():
        small = [pltpu.make_async_copy(a, b, wsem.at[k])
                 for k, (a, b) in enumerate(((vr_hbm, vr), (kr_hbm, kr), (rate_hbm, rate), (cnt_hbm, cnt)))]
        for c in small:
            c.start()

        def group(hbm, ref, g, sem, out=False):
            sl = pl.ds(pl.multiple_of(8 * g, 8), 8)
            a, b = hbm.at[:, sl, :], ref.at[g]
            return pltpu.make_async_copy(b, a, sem) if out else pltpu.make_async_copy(a, b, sem)

        for g in range(8):
            group(vib_hbm, vib, g, sems.at[0, g]).start()
            group(sp_hbm, sp, g, sems.at[1, g]).start()
        for c in small:
            c.wait()
        powers(vr, kr, va, sa, w_scr, w8_scr)
        v2 = vib.reshape(8 * 368, 128)
        s2 = sp.reshape(8 * 240, 128)
        vo2 = vo.reshape(8 * 368, 128)
        so2 = so.reshape(8 * 240, 128)

        for g in range(8):
            coefs(rate[8 * g : 8 * g + 8, :], group_counts(cnt, g), s_scr, 8 * g)

        def ready(g):
            group(vib_hbm, vib, g, sems.at[0, g]).wait()
            group(sp_hbm, sp, g, sems.at[1, g]).wait()

        def emit(g):
            group(vo_hbm, vo, g, osems.at[0, g], True).start()
            group(so_hbm, so, g, osems.at[1, g], True).start()

        def cf(g, k, j):
            at = 8 * g + 2 * k
            return jnp.concatenate([s_scr[j - 1, pl.ds(at, 1), :], s_scr[j - 1, pl.ds(at + 1, 1), :]], 1)

        def expand(g, k, slot):
            p_scr[slot] = jnp.dot(w_scr[...], split_stack(load_pair(v2, s2, g, k)), preferred_element_type=F32)

        def combine(g, k, slot):
            x = load_pair(v2, s2, g, k)
            y0 = x
            y1 = cf(g, k, 8) * x
            for j in range(1, 9):
                w = p_scr[slot, 80 * (j - 1) : 80 * j, :]
                if j < 8:
                    y0 = y0 + cf(g, k, j) * w
                y1 = y1 + cf(g, k, 8 + j) * w
            y_scr[slot] = y0
            y1_scr[slot] = jnp.concatenate([y1.astype(BF16), jnp.zeros((48, 256), BF16)], 0)

        def finish(g, k, slot):
            z = jnp.dot(w8_scr[...], y1_scr[slot], preferred_element_type=F32)
            out = cf(g, k, 17) * (y_scr[slot] + z)
            for h in range(2):
                part = out[:, 128 * h : 128 * h + 128]
                for m, o in enumerate(VO):
                    vo2[pl.ds(g * 368 + (o * 8 + 2 * k + h), 8, stride=8), :] = part[8 * m : 8 * m + 8, :]
                for m, o in enumerate(SO):
                    so2[pl.ds(g * 240 + (o * 8 + 2 * k + h), 8, stride=8), :] = part[48 + 8 * m : 56 + 8 * m, :]

        ready(0)
        expand(0, 0, 0)
        y_scr[1] = jnp.zeros((80, 256), F32)
        y1_scr[1] = jnp.zeros((128, 256), BF16)

        @pl.loop(0, 8)
        def _(g):
            pl.when(g < 7)(lambda: ready(g + 1))
            for k in range(4):
                expand(jnp.minimum(g + 1, 7) if k == 3 else g, (k + 1) % 4, (k + 1) % 2)
                finish(jnp.maximum(g - 1, 0) if k == 0 else g, (k - 1) % 4, (k + 1) % 2)
                combine(g, k, k % 2)
            pl.when(g > 0)(lambda: emit(g - 1))

        finish(7, 3, 1)
        emit(7)
        for g in range(8):
            group(vo_hbm, vo, g, osems.at[0, g], True).wait()
            group(so_hbm, so, g, osems.at[1, g], True).wait()


def chem(early, vib, sp, rate, cnt, vr, kr, extra):
    hbm = pl.BlockSpec(memory_space=pl.ANY)
    n = len(extra)
    like = lambda v: jax.ShapeDtypeStruct(v.shape, v.dtype)
    outs = [like(vib), like(sp)] + ([like(v) for v in extra] if early else [])
    out = pl.pallas_call(
        functools.partial(chem_kernel, early),
        in_specs=[hbm] * (6 + n),
        out_specs=[hbm] * len(outs),
        out_shape=outs,
        input_output_aliases={6 + k: k + (2 if early else 0) for k in range(n)},
        scratch_shapes=[pltpu.VMEM((46, 46), F32), pltpu.VMEM((30, 30), F32), pltpu.SMEM((64,), jnp.int32),
                        pltpu.VMEM((64, 128), F32)]
        + [pltpu.VMEM((8, k, 8, 128), F32) for k in (46, 30, 46, 30)]
        + [pltpu.VMEM((48, 128), F32), pltpu.VMEM((32, 128), F32),
           pltpu.VMEM((640, 256), BF16), pltpu.VMEM((80, 128), BF16),
           pltpu.VMEM((17, 64, 128), F32), pltpu.VMEM((2, 640, 256), F32),
           pltpu.VMEM((2, 80, 256), F32), pltpu.VMEM((2, 128, 256), BF16),
           pltpu.SemaphoreType.DMA((2, 8)), pltpu.SemaphoreType.DMA((2, 8)), pltpu.SemaphoreType.DMA((4,))],
        compiler_params=pltpu.CompilerParams(vmem_limit_bytes=62 * 2**20),
        cost_estimate=pl.CostEstimate(flops=10**9, bytes_accessed=6 * 10**6, transcendentals=0),
        name="chemistry_early" if early else "chemistry_late",
    )(vr, kr, cnt, rate, vib, sp, *extra)
    return out[:2], out[2:]


def cell_flux(q, d):
    inv = 1.0 / q[0]
    u = q[d] * inv
    p = 0.4 * (q[4] - 0.5 * (q[1] * q[1] + q[2] * q[2] + q[3] * q[3]) * inv)
    f = [q[d], q[1] * u, q[2] * u, q[3] * u, (q[4] + p) * u]
    f[d] = f[d] + p
    return f, jnp.abs(u) + jnp.sqrt(1.4 * p * inv)


def recip(v):
    return pl.reciprocal(v, approx=True)


def side(v2, d0, d1, d2, d3):
    c0, c1, c2 = d1 - d0, d2 - d1, d3 - d2
    t1 = 3.0 * d1
    e0 = t1 - d0
    e1 = d1 + d2
    e2 = d3 - 3.0 * d2
    k = 13.0 / 3.0
    s0 = 1.6e-5 + (k * (c0 * c0) + e0 * e0)
    s1 = 1.6e-5 + (k * (c1 * c1) + e1 * e1)
    s2 = 1.6e-5 + (k * (c2 * c2) + e2 * e2)
    r0, r1, r2 = recip(s0), recip(s1), recip(s2)
    a0 = r0 * r0
    a1 = 6.0 * (r1 * r1)
    a2 = 3.0 * (r2 * r2)
    num = a0 * ((c0 + c0) + t1) + a1 * (e1 + d2) + a2 * (d2 - e2)
    den = a0 + a1 + a2
    return v2 + num * recip(6.0 * den)


def face(f, q, alpha):
    fd = [f[k + 1] - f[k] for k in range(5)]
    qd = [alpha * (q[k + 1] - q[k]) for k in range(5)]
    plus = side(f[2] + alpha * q[2], *[fd[k] + qd[k] for k in range(4)])
    m = [qd[k] - fd[k] for k in range(5)]
    minus = side(f[3] - alpha * q[3], m[4], m[3], m[2], m[1])
    return plus + minus


def weno_kernel(flow_ref, e_ref, xb_ref, yb_ref, xa_ref, ya_ref, own_ref, out_ref, xq, xf, xs, xg):
    even_x = lax.axis_index("gx") % 2 == 0
    even_y = lax.axis_index("gy") % 2 == 0
    xa, xb, ya, yb = xa_ref[...], xb_ref[...], ya_ref[0:8, :], yb_ref[0:8, :]
    up, dn = jnp.where(even_x, xb, xa), jnp.where(even_x, xa, xb)
    lq, rq = jnp.where(even_y, yb, ya), jnp.where(even_y, ya, yb)
    for c in range(5):
        xq[c, 5:8, :] = up[3 * c : 3 * c + 3, :]
        xq[c, 8:72, :] = e_ref[...] if c == 4 else flow_ref[c]
        xq[c, 72:75, :] = dn[3 * c : 3 * c + 3, :]
    one = jnp.ones((5, 128), F32)
    for c in range(5):
        fill = one if c in (0, 4) else 0.0 * one
        xq[c, 0:5, :] = fill
        xq[c, 75:80, :] = fill
    for g in range(10):
        sl = slice(8 * g, 8 * g + 8)
        f, s = cell_flux([xq[c, sl, :] for c in range(5)], 1)
        for c in range(5):
            xf[c, sl, :] = f[c]
        xs[sl, :] = s
    for g in range(9):
        b = 8 * g + 5
        n = 8 if g < 8 else 1
        alpha = xs[b : b + n, :]
        for o in range(1, 6):
            alpha = jnp.maximum(alpha, xs[b + o : b + o + n, :])
        for c in range(5):
            xg[c, 8 * g : 8 * g + n, :] = face(
                [xf[c, b + o : b + o + n, :] for o in range(6)],
                [xq[c, b + o : b + o + n, :] for o in range(6)],
                alpha,
            )

    lane = lax.broadcasted_iota(jnp.int32, (8, 128), 1)
    slot = lane % 16

    def shift(v, k):
        return v if k % 128 == 0 else pltpu.roll(v, (-k) % 128, 1)

    def strip(v):
        q = [shift(v, 3 * c) for c in range(5)]
        f, s = cell_flux(q, 2)
        ff = f[0]
        ss = s
        for c in range(1, 5):
            here = slot >= 3 * c
            ff = jnp.where(here, shift(f[c], -3 * c), ff)
            ss = jnp.where(here, shift(s, -3 * c), ss)
        return v, ff, ss

    lq, lfx, ls = strip(lq)
    oq, ofx, os_ = strip(own_ref[...])
    alpha = ls
    for v in (shift(ls, 1), shift(ls, 2), os_, shift(os_, 1), shift(os_, 2)):
        alpha = jnp.maximum(alpha, v)
    first = face(
        [lfx, shift(lfx, 1), shift(lfx, 2), ofx, shift(ofx, 1), shift(ofx, 2)],
        [lq, shift(lq, 1), shift(lq, 2), oq, shift(oq, 1), shift(oq, 2)],
        alpha,
    )
    before_it = shift(lq, 3)
    both = [jnp.where((slot >= 3 * c) & (slot < 3 * c + 3), rq, before_it) for c in range(5)]
    for g in range(8):
        sl = slice(8 * g + 8, 8 * g + 16)
        q = [xq[c, sl, :] for c in range(5)]
        h = [shift(both[c], 16 * g + 3 * c) for c in range(5)]
        f, s = cell_flux(q, 2)
        hf, hs = cell_flux(h, 2)

        def six(a, b):
            out = []
            for o in range(-2, 4):
                if o == 0:
                    out.append(a)
                elif o > 0:
                    out.append(shift(jnp.where(lane < o, b, a), o))
                else:
                    out.append(shift(jnp.where(lane >= 128 + o, b, a), o))
            return out

        alphas = six(s, hs)
        alpha = alphas[0]
        for v in alphas[1:]:
            alpha = jnp.maximum(alpha, v)
        qs = [six(q[c], h[c]) for c in range(5)]
        for c in range(5):
            after = face(qs[2] if c == 0 else six(f[c], hf[c]), qs[c], alpha)
            before = jnp.where(lane == 0, shift(first, 16 * g + 3 * c), shift(after, -1))
            gx = xg[c, 8 * g + 1 : 8 * g + 9, :] - xg[c, 8 * g : 8 * g + 8, :]
            out_ref[c, 8 * g : 8 * g + 8, :] = q[c] - 0.05 * (gx + (after - before))


def weno(flow, e, xb, yb, xa, ya, own):
    vm = pl.BlockSpec(memory_space=pltpu.VMEM)
    return pl.pallas_call(
        weno_kernel,
        in_specs=[vm] * 7,
        out_specs=vm,
        out_shape=jax.ShapeDtypeStruct((5, 64, 128), F32),
        scratch_shapes=[pltpu.VMEM((5, 80, 128), F32), pltpu.VMEM((5, 80, 128), F32), pltpu.VMEM((80, 128), F32),
                        pltpu.VMEM((5, 72, 128), F32)],
        compiler_params=pltpu.CompilerParams(vmem_limit_bytes=20 * 2**20),
        cost_estimate=pl.CostEstimate(flops=10**7, bytes_accessed=10**6, transcendentals=0),
        name="euler_weno",
    )(flow, e, xb, yb, xa, ya, own)


def swaps(size, start):
    pairs = [(i % size, (i + 1) % size) for i in range(start, size, 2)]
    return pairs + [(b, a) for a, b in pairs]


def swapped(value, axis, start):
    return lax.ppermute(value, axis, swaps(lax.axis_size(axis), start))


def local(flow, vib, species, field_rate, substeps, vib_rates, kin_rates, level_energy, formation_heat):
    counts = substeps.reshape(-1)
    e, xa, xb, ya, yb, own = heat(
        flow, vib, species, field_rate, counts, vib_rates, kin_rates, level_energy, formation_heat
    )
    first, (xa, xb, ya, yb) = chem(
        True, vib, species, field_rate, counts, vib_rates, kin_rates, (xa, xb, ya, yb)
    )
    xb = swapped(xb, "gx", 1)
    yb = swapped(yb, "gy", 1)
    xa = swapped(xa, "gx", 0)
    ya = swapped(ya, "gy", 0)
    (vib_final, species_final), _ = chem(False, vib, species, field_rate, counts, vib_rates, kin_rates, first)
    return (weno(flow, e, xb, yb, xa, ya, own), vib_final, species_final)


def solution(mesh):
    tiled = P(None, "gx", "gy")
    return jax.shard_map(
        local,
        mesh=mesh,
        in_specs=(tiled, tiled, tiled, P("gx", "gy"), P("gx", "gy"), P(), P(), P(), P()),
        out_specs=(tiled, tiled, tiled),
        check_vma=False,
    )
```
